256 devices in a mesh: region: 128 (over x, y, z), member: 2 (over core).
Axes of the slice: x: 4, y: 4, z: 8, core: 2. Of those that a mesh axis runs over, the one named last changes fastest.
Arguments:
- ensemble: float32 [983040, 256], P('region', 'member'), may hold values from -6 to 6
- couplings: bfloat16 [15360, 4, 64, 64], P('region'), may hold values from -0.375 to 0.375
- neighbours: int32 [15360, 4], P('region'), may hold values from 0 to 124, as said below
- destination: int32 [15360], P('region'), may hold values from 0 to 127, as said below
- obs_index: int32 [128, 512], P('region'), may hold values from 0 to 8191, as said below
- obs_class: int32 [128, 512], P('region'), may hold values from 0 to 4
- obs_error: float32 [128, 512], P('region'), may hold values from 0.5 to 2
- obs_value: float32 [128, 512], P('region'), may hold values from -8 to 8
Outputs:
- posterior_ensemble: bfloat16 [983040, 256], P('region', 'member')
The draws below stay inside these ranges and needn't reach their ends.
Inputs may be any that keep to these rules, and one draw needn't show every extreme that they name: `neighbours`: entry 0 is the block itself (2 + i); entries 1 and 2 lie within 2 of it; entry 3 is within 2 of it or padding (124). Block 0 of every partition lists 0 and block 119 lists 120 + 2 * 2 - 1. `destination`: the blocks of one partition have distinct destinations, so at most 1 go from one partition to one region; some region receives a block in every one of its slots. `obs_index`: every observation reads a cell of a slot that holds a block.
All inputs are finite; a program needn't handle non-finite values.
Results may differ from the reference program's by a relative error of at most 0.0083.
Values may be sent and summed in bfloat16 or wider, within the bound.
A program may use at most 128 MiB of HBM per device.

```python
import math
import jax
import jax.numpy as jnp
from jax import lax

BLOCK_CELL_COUNT = 64
NBLK = 120
HALO = 2
NEIGHB = 4
MEMBERS = 256
REGION_READINGS = 512
ITERS = 4
PARTITION_SLOTS = 1
REGION_SLOTS = 128
GRID_TILES_ALL = 15360
CELLS = 983040
N_REGION = 128


def slot_choice(key):
    key_region, key_shuffle = jax.random.split(key)
    region_complete = jax.random.randint(key_region, (), 0, N_REGION)
    shuffled_blocks = jax.vmap(lambda subset_rows: jax.random.permutation(subset_rows, REGION_SLOTS))(jax.random.split(key_shuffle, N_REGION))
    region_lookup = jnp.arange(REGION_SLOTS, dtype=jnp.int32) // PARTITION_SLOTS
    ranking_values = shuffled_blocks.astype(jnp.int32) + jnp.where(region_lookup == region_complete, REGION_SLOTS, 0).astype(jnp.int32)[None, :]
    ranked = jnp.argsort(-ranking_values, axis=1, stable=True)
    return (ranked[:, :NBLK].astype(jnp.int32), region_complete)


def draw_destination(key, part):
    selected_slots, region_complete = slot_choice(key)
    return selected_slots.reshape(-1)


def draw_obs_index(key, part):
    selected_slots, region_complete = slot_choice(key)
    key = jax.random.fold_in(key, 7)
    key_slotpick, key_cell = jax.random.split(key)
    source_partitions = jnp.arange(N_REGION, dtype=jnp.int32)[:, None] * jnp.ones((1, NBLK), jnp.int32)
    active_slots = jnp.zeros((N_REGION, REGION_SLOTS), jnp.int32).at[source_partitions, selected_slots].set(1)
    active_region = active_slots.reshape(N_REGION, N_REGION, PARTITION_SLOTS).transpose(1, 0, 2).reshape(N_REGION, REGION_SLOTS)
    ranking_values = jax.random.randint(key_slotpick, (N_REGION, REGION_READINGS, REGION_SLOTS), 0, 1 << 20) + active_region[:, None, :] * (1 << 21)
    slot_pick = jnp.argmax(ranking_values, axis=-1).astype(jnp.int32)
    cell_pick = jax.random.randint(key_cell, (N_REGION, REGION_READINGS), 0, BLOCK_CELL_COUNT)
    reading_values = slot_pick * BLOCK_CELL_COUNT + cell_pick
    region_numbers = jnp.arange(N_REGION, dtype=jnp.int32)[:, None]
    reading_index = jnp.arange(REGION_READINGS, dtype=jnp.int32)[None, :]
    reading_values = jnp.where((region_numbers == region_complete) & (reading_index == 0), REGION_SLOTS * BLOCK_CELL_COUNT - 1, reading_values)
    reading_values = jnp.where((region_numbers == region_complete) & (reading_index == 1), 0, reading_values)
    return reading_values.astype(jnp.int32)


def draw_neighbours(key, part):
    key = jax.random.fold_in(key, 11)
    key_one, key_two, key_three, key_use = jax.random.split(key, 4)
    local_block = jnp.arange(GRID_TILES_ALL, dtype=jnp.int32) % NBLK
    first = local_block + HALO
    second = local_block + HALO + jax.random.randint(key_one, (GRID_TILES_ALL,), -HALO, HALO + 1)
    second = jnp.where(local_block == 0, 0, jnp.where(local_block == NBLK - 1, NBLK + 2 * HALO - 1, second))
    third = local_block + HALO + jax.random.randint(key_two, (GRID_TILES_ALL,), -HALO, HALO + 1)
    used = (jax.random.randint(key_use, (GRID_TILES_ALL,), 0, 2) == 1) & (local_block != 1)
    fourth = jnp.where(used, local_block + HALO + jax.random.randint(key_three, (GRID_TILES_ALL,), -HALO, HALO + 1), NBLK + 2 * HALO)
    return jnp.stack([first, second, third, fourth], axis=1).astype(jnp.int32)


def touch_ends(entries, own_key, least, largest):
    dims = entries.shape
    spot = [jax.random.randint(jax.random.fold_in(own_key, axis), (), 0, dims[axis]) for axis in range(len(dims))]
    entries = entries.at[tuple(spot)].set(least)
    longest = dims.index(max(dims))
    spot[longest] = (spot[longest] + 1) % dims[longest]
    return entries.at[tuple(spot)].set(largest)


def shard_levels(own_key, extent, cuts, low, largest):
    def one(dim, parts):
        heights = jax.random.uniform(jax.random.fold_in(jax.random.fold_in(own_key, 6), dim), (parts,), jnp.float32, low / len(cuts), largest / len(cuts))
        return jnp.repeat(jnp.exp(heights), extent[dim] // parts).reshape((-1,) + (1,) * (len(extent) - dim - 1))

    gain = one(*cuts[0])
    for cut in cuts[1:]:
        gain = gain * one(*cut)
    return gain


def normal_values(rng, extent, width, reach, cuts=(), kind=jnp.bfloat16):
    values = width * jax.random.normal(rng, extent, jnp.float32)
    if cuts:
        values = values * shard_levels(rng, extent, cuts, -0.22, 0.18)
    return jnp.clip(values, -reach, reach).astype(kind)


def setup_inputs(seed: int = 0) -> dict:
    keys = jax.random.split(jax.random.key(seed), 9)
    ensemble = normal_values(keys[0], (CELLS, MEMBERS), 1.0, 6.0, ((0, 128), (1, 2)), jnp.float32)
    couplings = normal_values(keys[1], (GRID_TILES_ALL, NEIGHB, BLOCK_CELL_COUNT, BLOCK_CELL_COUNT), (NEIGHB * BLOCK_CELL_COUNT) ** -0.5, 0.375, ((0, 128),))
    neighbours = draw_neighbours(jax.random.fold_in(keys[8], 71), 0)
    destination = draw_destination(jax.random.fold_in(keys[8], 71), 0)
    obs_index = draw_obs_index(jax.random.fold_in(keys[8], 71), 0)
    obs_class = touch_ends(jax.random.randint(keys[5], (N_REGION, REGION_READINGS), 0, 5), jax.random.fold_in(keys[5], 1), 0, 4).astype(jnp.int32)
    obs_error = jnp.clip(jnp.exp(math.log(2.0) - 1.3862944 * jax.random.uniform(keys[6], (N_REGION, REGION_READINGS), jnp.float32) ** shard_levels(keys[6], (N_REGION, REGION_READINGS), ((0, 128),), -0.2, 0.2)), 0.5, 2.0)
    obs_value = normal_values(keys[7], (N_REGION, REGION_READINGS), 2.0, 8.0, ((0, 128),), jnp.float32)
    return dict(ensemble=ensemble, couplings=couplings, neighbours=neighbours, destination=destination, obs_index=obs_index, obs_class=obs_class, obs_error=obs_error, obs_value=obs_value)


def newton(system):
    identity = jnp.eye(system.shape[0], dtype=jnp.float32)
    iterate = system
    inverse = identity
    for sweep in range(ITERS):
        update = 1.5 * identity - 0.5 * jnp.dot(inverse, iterate, precision=lax.Precision.HIGHEST)
        iterate = jnp.dot(iterate, update, precision=lax.Precision.HIGHEST)
        inverse = jnp.dot(update, inverse, precision=lax.Precision.HIGHEST)
    return inverse

def analyse(rows_per_slot, obs_rows, obs_cls, obs_err, obs_val):
    member_states = rows_per_slot.shape[1]
    identity = jnp.eye(member_states, dtype=jnp.float32)
    cell_mean = lax.optimization_barrier(jnp.sum(rows_per_slot.astype(jnp.float32), axis=1)) / member_states
    deviation = (rows_per_slot.astype(jnp.float32) - cell_mean[:, None]).astype(jnp.bfloat16)
    obs_pert = deviation[obs_rows].astype(jnp.float32)
    departure = obs_val - cell_mean[obs_rows]
    weight = jnp.maximum(0.0, 1.0 - 0.25 * obs_cls.astype(jnp.float32)) / obs_err
    gram_matrix = jnp.dot(obs_pert.T, obs_pert * weight[:, None], precision=lax.Precision.HIGHEST)
    system = (member_states - 1.0) * identity + gram_matrix
    frob_scale = jnp.sqrt(jnp.sum(system * system))
    root_inv = newton(system / frob_scale) / jnp.sqrt(frob_scale)
    innov_proj = jnp.dot(obs_pert.T, weight * departure, precision=lax.Precision.HIGHEST)
    mean_weights = jnp.dot(root_inv, jnp.dot(root_inv, innov_proj, precision=lax.Precision.HIGHEST), precision=lax.Precision.HIGHEST)
    combined = (mean_weights[:, None] + jnp.sqrt(member_states - 1.0) * root_inv - identity).astype(jnp.bfloat16)
    return jnp.dot(deviation, combined, preferred_element_type=jnp.float32).astype(jnp.bfloat16)

def reference(ensemble, couplings, neighbours, destination, obs_index, obs_class, obs_error, obs_value):
    member_states = ensemble.shape[1]
    prognostic_vector = ensemble.reshape(GRID_TILES_ALL, BLOCK_CELL_COUNT, member_states)
    coupled = couplings.reshape(N_REGION, NBLK, NEIGHB, BLOCK_CELL_COUNT, BLOCK_CELL_COUNT)
    lists = neighbours.reshape(N_REGION, NBLK, NEIGHB)
    owner = jnp.arange(N_REGION, dtype=jnp.int32)
    pad_entry = NBLK + 2 * HALO
    padded_index = jnp.where(lists == pad_entry, GRID_TILES_ALL + 2 * HALO, owner[:, None, None] * NBLK + lists).astype(jnp.int32)

    def propagate_tiles(field_now):
        rounded = field_now.astype(jnp.bfloat16)
        zero_rim = jnp.zeros((HALO, BLOCK_CELL_COUNT, member_states), jnp.bfloat16)
        padded = jnp.concatenate([zero_rim, rounded, zero_rim, jnp.zeros((1, BLOCK_CELL_COUNT, member_states), jnp.bfloat16)], axis=0)

        def route_owner(pair):
            coeffs, where_from = pair
            picked = padded[where_from]
            return jnp.einsum('ijcd,ijdk->ick', coeffs.astype(jnp.float32), picked.astype(jnp.float32))
        return lax.map(route_owner, (coupled, padded_index)).reshape(GRID_TILES_ALL, BLOCK_CELL_COUNT, member_states)
    prior_vector = propagate_tiles(propagate_tiles(prognostic_vector))
    sent_tile_lines = prior_vector.astype(jnp.bfloat16)
    block_ids = jnp.arange(GRID_TILES_ALL, dtype=jnp.int32)
    block_per_slot = jnp.full((N_REGION, REGION_SLOTS), GRID_TILES_ALL, jnp.int32)
    block_per_slot = block_per_slot.at[destination // PARTITION_SLOTS, block_ids // NBLK * PARTITION_SLOTS + destination % PARTITION_SLOTS].set(block_ids)
    blocks_extended = jnp.concatenate([sent_tile_lines, jnp.zeros((1, BLOCK_CELL_COUNT, member_states), jnp.bfloat16)], axis=0)

    def one_region(region_id, summed_correction):
        selected_slots = block_per_slot[region_id]
        rows_per_slot = blocks_extended[selected_slots].reshape(REGION_SLOTS * BLOCK_CELL_COUNT, member_states)
        state_increment = analyse(rows_per_slot, obs_index[region_id], obs_class[region_id], obs_error[region_id], obs_value[region_id])
        return summed_correction.at[selected_slots].set(state_increment.reshape(REGION_SLOTS, BLOCK_CELL_COUNT, member_states))
    summed_correction = lax.fori_loop(0, N_REGION, one_region, jnp.zeros((GRID_TILES_ALL + 1, BLOCK_CELL_COUNT, member_states), jnp.bfloat16))
    posterior_ensemble = (prior_vector + summed_correction[:GRID_TILES_ALL].astype(jnp.float32)).astype(jnp.bfloat16)
    return posterior_ensemble.reshape(CELLS, member_states)
```

```python
import functools
import jax
import jax.numpy as jnp
from jax import lax
from jax.experimental import pallas as pl
from jax.experimental.pallas import tpu as pltpu
from jax.sharding import PartitionSpec as P

MESH = pl.DeviceIdType.MESH
NX, NY, NZ = 4, 4, 8
NQ = NX * NY
REGIONS = NQ * NZ
BLOCKS = 120
CELLS = 64
OWN = 128
MEMBERS = 256
OBS = 512
NEIGHB = 4
ITERS = 4
ROWS = NQ * CELLS
GROUP = 8
HALO = 2
WINDOW = 8
PART = OWN + 16
CHUNKS = ROWS // OWN
F32 = jnp.float32
BF16 = jnp.bfloat16
SHIFTS = sorted(
    [(a, b) for a in range(NX) for b in range(NY) if (a, b) != (0, 0)],
    key=lambda s: min(s[0], NX - s[0]) + min(s[1], NY - s[1]),
)


def depth_shift(k):
    return 4 + (1 - 2 * (k % 2)) * ((k + 1) // 2)


def bfdot(a, b):
    return jnp.dot(a, b, preferred_element_type=F32)


def halves(a):
    hi = a.astype(BF16)
    return hi, (a - hi.astype(F32)).astype(BF16)


def matmul(a, b):
    return bfdot(a[0], b[0]) + bfdot(a[0], b[1]) + bfdot(a[1], b[0])


def kernel(
    nbr, nbr_rows, dest, dest_row, ens_hbm, cpl_hbm, obs_index, obs_class, obs_error, obs_value, out,
    inv, inv_rows, ens, raw, turned_cpl, cmat, own0, low, high, ext1, cmat_far, nbr_send, nbr_recv, nbr_far, fc, send, recv, sib, po, ps, ret_send, ret_recv,
    vu_send, vu_recv, part_send, part_recv, mx_send, mx_recv, g_recv,
    ens_sem, cpl_sem, inv_sem, far_sem, halo_send, halo_recv, a_send, a_recv, sx_send, sx_recv,
    vu_ssem, vu_rsem, p_ssem, p_rsem, m_ssem, m_rsem, g_ssem, g_rsem, r_ssem, r_rsem,
):
    me = lax.axis_index("region")
    core = lax.axis_index("member")
    q_me = me // NZ
    z = me % NZ
    x = q_me // NY
    y = q_me % NY

    def plane_peer(dx, dy):
        return ((x + dx) % NX) * NY + (y + dy) % NY

    def remote(src, dst, ssem, rsem, region, member):
        return pltpu.make_async_remote_copy(
            src_ref=src, dst_ref=dst, send_sem=ssem, recv_sem=rsem,
            device_id=(region, member), device_id_type=MESH,
        )

    right = (me + 1) % REGIONS
    left = (me + REGIONS - 1) % REGIONS

    edges = [(0, GROUP), (BLOCKS - GROUP, GROUP), (GROUP, BLOCKS - 2 * GROUP)]
    ens_copies = [
        pltpu.make_async_copy(ens_hbm.at[pl.ds(a, n)], ens.at[pl.ds(a, n)], ens_sem.at[i])
        for i, (a, n) in enumerate(edges)
    ]
    for c in ens_copies[:2]:
        c.start()
    cpl_copies = [
        pltpu.make_async_copy(cpl_hbm.at[j], raw.at[j], cpl_sem.at[j]) for j in range(NEIGHB)
    ]
    for c in cpl_copies + ens_copies[2:]:
        c.start()

    barrier = pltpu.get_barrier_semaphore()
    peers = [(plane_peer(dx, dy) * NZ + z, core) for dx, dy in SHIFTS]
    peers += [(q_me * NZ + (z + d) % NZ, core) for d in range(1, NZ)]
    peers += [(me, 1 - core), (right, core), (left, core)]
    for p in peers:
        pl.semaphore_signal(barrier, 1, device_id=p, device_id_type=MESH)
    zero_block = jnp.zeros((1, CELLS, OWN), BF16)
    own0[pl.ds(BLOCKS, 1)] = zero_block
    low[pl.ds(WINDOW, 1)] = zero_block
    high[pl.ds(WINDOW, 1)] = zero_block
    ext1[pl.ds(BLOCKS + 4, 1)] = zero_block

    hit = lax.broadcasted_iota(jnp.int32, (REGIONS, BLOCKS), 0) == dest_row[...]
    numbers = (lax.broadcasted_iota(jnp.int32, (8, BLOCKS), 1) + 1).astype(F32).astype(BF16)
    found = lax.dot_general(
        numbers, jnp.where(hit, 1.0, 0.0).astype(BF16), (((1,), (1,)), ((), ())),
        preferred_element_type=F32,
    )
    inv_rows[...] = jnp.minimum(found, float(BLOCKS)).astype(jnp.int32) - 1
    inv_copy = pltpu.make_async_copy(inv_rows, inv, inv_sem)
    inv_copy.start()

    def cast(a, n):
        own0[pl.ds(a, n)] = ens[pl.ds(a, n)].astype(BF16)

    def to_sides(i, upper, lower, from_left, from_right):
        return [
            remote(upper, from_left, halo_send.at[2 * i], halo_recv.at[2 * i], right, core),
            remote(lower, from_right, halo_send.at[2 * i + 1], halo_recv.at[2 * i + 1], left, core),
        ]

    ens_copies[0].wait()
    cast(0, GROUP)
    ens_copies[1].wait()
    cast(BLOCKS - GROUP, GROUP)
    pl.semaphore_wait(barrier, len(peers))
    nbr_send[...] = jnp.zeros_like(nbr_send)
    nbr_send[0:NEIGHB, 0:BLOCKS] = nbr_rows[...]
    sides = to_sides(0, own0.at[pl.ds(BLOCKS - 4, 4)], own0.at[pl.ds(0, 4)],
                     low.at[pl.ds(0, 4)], high.at[pl.ds(4, 4)])
    lists = to_sides(1, nbr_send, nbr_send, nbr_recv.at[0], nbr_recv.at[1])
    for c in sides + lists:
        c.start()
    low[pl.ds(4, 4)] = own0[pl.ds(0, 4)]
    high[pl.ds(0, 4)] = own0[pl.ds(BLOCKS - 4, 4)]

    for pair in range(NEIGHB // 2):
        cpl_copies[2 * pair].wait()
        cpl_copies[2 * pair + 1].wait()

        @pl.loop(0, CELLS // GROUP)
        def _(g):
            for t in range(GROUP):
                c = g * GROUP + t
                slab = raw[pl.ds(2 * pair, 2), c].reshape(2 * CELLS, BLOCKS)
                turned_cpl[pair, pl.ds(pl.multiple_of(c * BLOCKS, 8), BLOCKS)] = slab.T.astype(F32)

    ens_copies[2].wait()

    @pl.loop(1, BLOCKS // GROUP - 1)
    def _(g):
        cast(g * GROUP, GROUP)


    def couple(i):
        cmat[i] = jnp.concatenate(
            [turned_cpl[pair, pl.ds(i, CELLS, stride=BLOCKS)] for pair in range(NEIGHB // 2)],
            axis=1,
        ).astype(BF16)

    def route(coeff, ext, places):
        return bfdot(coeff, jnp.concatenate([ext[p] for p in places], axis=0))

    for i in (0, 1, BLOCKS - 2, BLOCKS - 1):
        couple(i)
    coeffs = to_sides(2, cmat.at[pl.ds(BLOCKS - 2, 2)], cmat.at[pl.ds(0, 2)],
                      cmat_far.at[pl.ds(0, 2)], cmat_far.at[pl.ds(2, 2)])
    for c in coeffs:
        c.start()

    def inner(i):
        couple(i)
        places = [jnp.clip(nbr[j, i] - HALO, 0, BLOCKS) for j in range(NEIGHB)]
        ext1[i + HALO] = route(cmat[i], own0, places).astype(BF16)

    @pl.loop(0, (BLOCKS - 4) // GROUP)
    def _(g):
        for t in range(GROUP):
            inner(HALO + g * GROUP + t)

    for i in range(HALO + (BLOCKS - 4) // GROUP * GROUP, BLOCKS - HALO):
        inner(i)

    for c in lists:
        c.wait()
    far_copy = pltpu.make_async_copy(nbr_recv, nbr_far, far_sem)
    far_copy.start()
    for c in sides:
        c.wait()

    @pl.when(me == 0)
    def _():
        low[pl.ds(0, 4)] = jnp.zeros((4, CELLS, OWN), BF16)

    @pl.when(me == REGIONS - 1)
    def _():
        high[pl.ds(4, 4)] = jnp.zeros((4, CELLS, OWN), BF16)

    def first(e):
        return jnp.clip(e + 2, 0, WINDOW)

    def final(e):
        return jnp.clip(jnp.where(e == BLOCKS + 2 * HALO, WINDOW, e - (BLOCKS - 2)), 0, WINDOW)

    for t in range(HALO):
        i = BLOCKS - HALO + t
        places = [first(nbr[j, t]) for j in range(NEIGHB)]
        ext1[t + HALO] = route(cmat[t], low, places).astype(BF16)
        places = [final(nbr[j, i]) for j in range(NEIGHB)]
        ext1[i + HALO] = route(cmat[i], high, places).astype(BF16)
    for c in coeffs:
        c.wait()
    far_copy.wait()
    for t in range(HALO):
        i = BLOCKS - HALO + t
        places = [final(nbr_far[0, j, i]) for j in range(NEIGHB)]
        ext1[t] = route(cmat_far[t], low, places).astype(BF16)
        places = [first(nbr_far[1, j, t]) for j in range(NEIGHB)]
        ext1[BLOCKS + HALO + t] = route(cmat_far[HALO + t], high, places).astype(BF16)

    @pl.when(me == 0)
    def _():
        ext1[pl.ds(0, HALO)] = jnp.zeros((HALO, CELLS, OWN), BF16)

    @pl.when(me == REGIONS - 1)
    def _():
        ext1[pl.ds(BLOCKS + HALO, HALO)] = jnp.zeros((HALO, CELLS, OWN), BF16)

    inv_copy.wait()

    @pl.loop(0, NZ)
    def _(k):
        zr = (z + depth_shift(k)) % NZ
        for q in range(NQ):
            r = q * NZ + zr
            b = inv[0, r]
            held = jnp.clip(b, 0, BLOCKS - 1)
            field = route(cmat[held], ext1, [nbr[j, held] for j in range(NEIGHB)])
            field = jnp.where(b >= 0, field, 0.0)
            fc[r] = field
            send[k, q] = field.astype(BF16)
        recv[k, q_me] = send[k, q_me]
        for dx, dy in SHIFTS:
            to = plane_peer(dx, dy)
            remote(send.at[k, to], recv.at[k, q_me], a_send.at[k], a_recv.at[k],
                   to * NZ + z, core).start()

    index = obs_index[...]
    weight = jnp.maximum(0.0, 1.0 - 0.25 * obs_class[...].astype(F32)) / obs_error[...]
    value = weight * obs_value[...]
    place = (index // (CELLS * NZ)) * CELLS + index % CELLS
    plane = (index // CELLS) % NZ
    plane_hit = lax.broadcasted_iota(jnp.int32, (NZ, OBS), 0) == plane

    def three(a):
        hi = a.astype(BF16).astype(F32)
        mid = (a - hi).astype(BF16).astype(F32)
        low = a - hi - mid
        return [hi, mid, low]

    pieces = three(weight) + three(value)
    lhs = jnp.concatenate([jnp.where(plane_hit, p, 0.0) for p in pieces], axis=0).astype(BF16)
    cell_hit = jnp.where(
        lax.broadcasted_iota(jnp.int32, (ROWS, OBS), 0) == place, 1.0, 0.0
    ).astype(BF16)
    sums = lax.dot_general(lhs, cell_hit, (((1,), (1,)), ((), ())), preferred_element_type=F32)
    v_all = sums[0:NZ] + sums[NZ:2 * NZ] + sums[2 * NZ:3 * NZ]
    u_all = sums[3 * NZ:4 * NZ] + sums[4 * NZ:5 * NZ] + sums[5 * NZ:6 * NZ]
    for p in range(NZ):
        for c in range(CHUNKS):
            lanes = slice(c * OWN, (c + 1) * OWN)
            vu_send[p, c:c + 1] = v_all[p:p + 1, lanes]
            vu_send[p, CHUNKS + c:CHUNKS + c + 1] = u_all[p:p + 1, lanes]
    vu_recv[NZ - 1] = vu_send[z]

    @pl.loop(0, NZ - 1)
    def _(k):
        to = (z + NZ - depth_shift(k)) % NZ
        remote(vu_send.at[to], vu_recv.at[k], vu_ssem.at[k], vu_rsem.at[k],
               q_me * NZ + to, core).start()

    ones = jnp.ones((OWN, OWN), BF16)
    eye = (lax.broadcasted_iota(jnp.int32, (OWN, OWN), 0)
           == lax.broadcasted_iota(jnp.int32, (OWN, OWN), 1))

    def start_exchange(k):
        pltpu.make_async_copy(
            recv.at[k, pl.ds(0, NQ - 1)], recv.at[k, pl.ds(0, NQ - 1)], a_recv.at[k]
        ).wait()
        remote(recv.at[k], sib.at[k], sx_send.at[k], sx_recv.at[k], me, 1 - core).start()

    @pl.loop(0, NZ)
    def _(k):
        start_exchange(k)
        own = recv[k].reshape(ROWS, OWN)
        total = bfdot(own, ones)
        remote(recv.at[k], sib.at[k], sx_send.at[k], sx_recv.at[k], me, 1 - core).wait()
        other = sib[k].reshape(ROWS, OWN)
        mean = (total + bfdot(other, ones)) * (1.0 / MEMBERS)
        p_own = (own.astype(F32) - mean).astype(BF16)
        p_other = (other.astype(F32) - mean).astype(BF16)
        po[k] = p_own
        ps[k] = p_other
        mean_row = jnp.concatenate(
            [
                jnp.sum(jnp.where(eye, mean[c * OWN:(c + 1) * OWN], 0.0), axis=0, keepdims=True)
                for c in range(ROWS // OWN)
            ],
            axis=1,
        )

        @pl.when(k < NZ - 1)
        def _():
            pltpu.make_async_copy(vu_recv.at[k], vu_recv.at[k], vu_rsem.at[k]).wait()

        vu = vu_recv[k]
        v_row = jnp.concatenate([vu[c:c + 1] for c in range(CHUNKS)], axis=1)
        u_row = jnp.concatenate([vu[CHUNKS + c:CHUNKS + c + 1] for c in range(CHUNKS)], axis=1)
        turned = p_own.astype(F32).T
        scaled = (turned * v_row).astype(BF16)
        part_send[k, 0:OWN, 0:OWN] = bfdot(scaled, p_own).astype(BF16)
        part_send[k, 0:OWN, OWN:] = bfdot(scaled, p_other).astype(BF16)
        d_row = u_row - v_row * mean_row
        d_hi = d_row.astype(BF16).astype(F32)
        d_low = d_row - d_hi
        rows16 = lax.broadcasted_iota(jnp.int32, (16, ROWS), 0)
        d_rows = jnp.where(rows16 == 0, d_hi, jnp.where(rows16 == 1, d_low, 0.0)).astype(BF16)

        def tail(p):
            t = jnp.sum(bfdot(d_rows, p), axis=0, keepdims=True)
            hi = t.astype(BF16).astype(F32)
            rows = lax.broadcasted_iota(jnp.int32, (16, OWN), 0)
            return jnp.where(rows == 0, hi, jnp.where(rows == 1, t - hi, 0.0)).astype(BF16)

        part_send[k, OWN:, 0:OWN] = tail(p_own)
        part_send[k, OWN:, OWN:] = tail(p_other)

        @pl.when(k < NZ - 1)
        def _():
            remote(part_send.at[k], part_recv.at[k], p_ssem.at[k], p_rsem.at[k],
                   q_me * NZ + (z + depth_shift(k)) % NZ, core).start()

    total = part_send[NZ - 1].astype(F32)
    for k in range(NZ - 1):
        pltpu.make_async_copy(part_recv.at[k], part_recv.at[k], p_rsem.at[k]).wait()
        total = total + part_recv[k].astype(F32)
    mx_send[...] = total[0:OWN]
    swap = remote(mx_send, mx_recv, m_ssem, m_rsem, me, 1 - core)
    swap.start()
    innov = jnp.sum(total[OWN:], axis=0, keepdims=True)
    swap.wait()
    crossed = mx_recv[...]
    gram = jnp.concatenate(
        [total[0:OWN], jnp.concatenate([crossed[:, OWN:], crossed[:, :OWN]], axis=1)], axis=0
    )
    identity = jnp.where(
        lax.broadcasted_iota(jnp.int32, (MEMBERS, MEMBERS), 0)
        == lax.broadcasted_iota(jnp.int32, (MEMBERS, MEMBERS), 1), 1.0, 0.0,
    )
    system = (MEMBERS - 1.0) * identity + gram
    frob = jnp.sqrt(jnp.sum(jnp.sum(system * system, axis=0, keepdims=True), axis=1, keepdims=True))
    scaled = system * (1.0 / frob)
    update = 1.5 * identity - 0.5 * scaled
    inverse = halves(update)
    iterate = halves(matmul(halves(scaled), inverse))
    for sweep in range(1, ITERS):
        update = halves(1.5 * identity - 0.5 * matmul(inverse, iterate))
        if sweep < ITERS - 1:
            iterate = halves(matmul(iterate, update))
        last = matmul(update, inverse)
        inverse = halves(last)
    root = last * lax.rsqrt(frob)
    innov8 = jnp.broadcast_to(innov, (8, MEMBERS))
    mean_row = matmul(halves(matmul(halves(innov8), inverse)), inverse)[0:1] * (1.0 / frob)
    mean_col = jnp.broadcast_to(mean_row, (OWN, MEMBERS)).T
    g_recv[NZ - 1] = (
        mean_col + jnp.sqrt(MEMBERS - 1.0) * root[:, 0:OWN] - identity[:, 0:OWN]
    ).astype(BF16)

    def send_weights(k):
        remote(g_recv.at[NZ - 1], g_recv.at[k], g_ssem.at[k], g_rsem.at[k],
               q_me * NZ + (z + NZ - depth_shift(k)) % NZ, core).start()

    send_weights(NZ - 2)
    send_weights(NZ - 3)

    @pl.loop(0, NZ)
    def _(i):
        k = NZ - 1 - i

        @pl.when(k < NZ - 1)
        def _():
            pltpu.make_async_copy(g_recv.at[k], g_recv.at[k], g_rsem.at[k]).wait()

        g = g_recv[k]
        incr = bfdot(po[k], g[0:OWN]) + bfdot(ps[k], g[OWN:])
        ret_send[k] = incr.astype(BF16).reshape(NQ, CELLS, OWN)
        r = q_me * NZ + (z + depth_shift(k)) % NZ
        ret_recv[r] = ret_send[k, q_me]
        for dx, dy in SHIFTS:
            to = plane_peer(dx, dy)
            remote(ret_send.at[k, to], ret_recv.at[r], r_ssem, r_rsem, to * NZ + z, core).start()

        @pl.when(i < 2)
        def _():
            send_weights(NZ - 4 - 2 * i)
            send_weights(NZ - 5 - 2 * i)

        @pl.when(i == 2)
        def _():
            send_weights(0)

    count = NZ * (NQ - 1)
    done = ret_recv.at[pl.ds(0, count)]
    pltpu.make_async_copy(done, done, r_rsem).wait()

    @pl.loop(0, BLOCKS // GROUP)
    def _(g):
        for t in range(GROUP):
            i = g * GROUP + t
            r = dest[i]
            out[i] = (fc[r] + ret_recv[r].astype(F32)).astype(BF16)

    pltpu.make_async_copy(done, done, r_ssem).wait()

    @pl.loop(0, NZ)
    def _(k):
        block = send.at[k, pl.ds(0, NQ - 1)]
        pltpu.make_async_copy(block, block, a_send.at[k]).wait()

        @pl.when(k < NZ - 1)
        def _():
            pltpu.make_async_copy(vu_send.at[k], vu_send.at[k], vu_ssem.at[k]).wait()
            pltpu.make_async_copy(part_send.at[k], part_send.at[k], p_ssem.at[k]).wait()
            pltpu.make_async_copy(g_recv.at[k], g_recv.at[k], g_ssem.at[k]).wait()


def shards(
    ensemble, couplings, neighbours, destination, obs_index, obs_class, obs_error, obs_value
):
    smem = pl.BlockSpec(memory_space=pltpu.SMEM)
    vmem = pl.BlockSpec(memory_space=pltpu.VMEM)
    hbm = pl.BlockSpec(memory_space=pl.ANY)
    dma = pltpu.SemaphoreType.DMA
    block = (CELLS, OWN)
    posterior = pl.pallas_call(
        kernel,
        out_shape=pltpu.VMEM((BLOCKS,) + block, BF16),
        in_specs=[smem, vmem, smem, vmem, hbm, hbm, vmem, vmem, vmem, vmem],
        out_specs=vmem,
        scratch_shapes=[
            pltpu.SMEM((8, REGIONS), jnp.int32),
            pltpu.VMEM((8, REGIONS), jnp.int32),
            pltpu.VMEM((BLOCKS,) + block, F32),
            pltpu.VMEM((NEIGHB, CELLS, CELLS, BLOCKS), BF16),
            pltpu.VMEM((NEIGHB // 2, (CELLS + 1) * BLOCKS, 2 * CELLS), F32),
            pltpu.VMEM((BLOCKS, CELLS, NEIGHB * CELLS), BF16),
            pltpu.VMEM((BLOCKS + 1,) + block, BF16),
            pltpu.VMEM((WINDOW + 1,) + block, BF16),
            pltpu.VMEM((WINDOW + 1,) + block, BF16),
            pltpu.VMEM((BLOCKS + 5,) + block, BF16),
            pltpu.VMEM((2 * HALO, CELLS, NEIGHB * CELLS), BF16),
            pltpu.VMEM((8, REGIONS), jnp.int32),
            pltpu.VMEM((2, 8, REGIONS), jnp.int32),
            pltpu.SMEM((2, 8, REGIONS), jnp.int32),
            pltpu.VMEM((REGIONS,) + block, F32),
            pltpu.VMEM((NZ, NQ) + block, BF16),
            pltpu.VMEM((NZ, NQ) + block, BF16),
            pltpu.VMEM((NZ, NQ) + block, BF16),
            pltpu.VMEM((NZ, ROWS, OWN), BF16),
            pltpu.VMEM((NZ, ROWS, OWN), BF16),
            pltpu.VMEM((NZ, NQ) + block, BF16),
            pltpu.VMEM((REGIONS,) + block, BF16),
            pltpu.VMEM((NZ, 2 * CHUNKS, OWN), F32),
            pltpu.VMEM((NZ, 2 * CHUNKS, OWN), F32),
            pltpu.VMEM((NZ, PART, MEMBERS), BF16),
            pltpu.VMEM((NZ - 1, PART, MEMBERS), BF16),
            pltpu.VMEM((OWN, MEMBERS), F32),
            pltpu.VMEM((OWN, MEMBERS), F32),
            pltpu.VMEM((NZ, MEMBERS, OWN), BF16),
            dma((3,)), dma((NEIGHB,)), dma, dma, dma((6,)), dma((6,)),
            dma((NZ,)), dma((NZ,)), dma((NZ,)), dma((NZ,)),
            dma((NZ,)), dma((NZ,)), dma((NZ,)), dma((NZ,)),
            dma, dma, dma((NZ,)), dma((NZ,)), dma, dma,
        ],
        compiler_params=pltpu.CompilerParams(
            collective_id=0, has_side_effects=True, vmem_limit_bytes=58 << 20
        ),
        cost_estimate=pl.CostEstimate(
            flops=4_000_000_000, bytes_accessed=16_000_000, transcendentals=0
        ),
    )(
        neighbours.T, neighbours.T, destination, destination.reshape(1, BLOCKS), ensemble.reshape((BLOCKS,) + block),
        jnp.transpose(couplings, (1, 2, 3, 0)), obs_index, obs_class, obs_error, obs_value,
    )
    return posterior.reshape(BLOCKS * CELLS, OWN)


def solution(mesh):
    return jax.shard_map(
        shards,
        mesh=mesh,
        in_specs=(
            P("region", "member"),
            P("region", None, None, None),
            P("region", None),
            P("region"),
            P("region", None),
            P("region", None),
            P("region", None),
            P("region", None),
        ),
        out_specs=P("region", "member"),
        check_vma=False,
    )
```

```python
import functools
import jax
import jax.numpy as jnp
from jax import lax
from jax.experimental import pallas as pl
from jax.experimental.pallas import tpu as pltpu
from jax.sharding import PartitionSpec as P

MESH = pl.DeviceIdType.MESH
NX, NY, NZ = 4, 4, 8
NQ = NX * NY
REGIONS = NQ * NZ
BLOCKS = 120
CELLS = 64
OWN = 128
MEMBERS = 256
OBS = 512
NEIGHB = 4
ITERS = 4
ROWS = NQ * CELLS
GROUP = 8
HALF = NZ // 2
HALO = 2
WINDOW = 8
LISTS_AT = 11
PART = OWN + 16
CHUNKS = ROWS // OWN
F32 = jnp.float32
BF16 = jnp.bfloat16
SHIFTS = sorted(
    [(a, b) for a in range(NX) for b in range(NY) if (a, b) != (0, 0)],
    key=lambda s: min(s[0], NX - s[0]) + min(s[1], NY - s[1]),
)


def depth_shift(step, z):
    i = NZ - 1 - step
    t = i % HALF
    far = i // HALF
    half = z // HALF
    p = z % HALF
    up = p // 2
    near_place = (p + (1 - 2 * up) * t + HALF) % HALF
    far_place = (1 - up) * (HALF - 1 - t) + up * t
    place = (1 - far) * (half * HALF + near_place) + far * ((1 - half) * HALF + far_place)
    return (place - z + NZ) % NZ


def bfdot(a, b):
    return jnp.dot(a, b, preferred_element_type=F32)


def halves(a):
    hi = a.astype(BF16)
    return hi, (a - hi.astype(F32)).astype(BF16)


def matmul(a, b):
    return bfdot(
        jnp.concatenate([a[0], a[0], a[1]], axis=1), jnp.concatenate([b[0], b[1], b[0]], axis=0)
    )


def kernel(
    nbr, nbr_rows, dest, dest_row, ens_hbm, cpl_hbm, obs_index, obs_class, obs_error, obs_value, out,
    inv, inv_rows, ens, raw, turned_cpl, cmat, own0, low, high, ext1, cmat_far, nbr_send, nbr_recv, nbr_far, fc, send, recv, sib, po, ps, ret_send, ret_recv,
    vu_send, vu_recv, part_send, part_recv, mx_send, mx_recv, g_recv,
    ens_sem, cpl_sem, inv_sem, far_sem, halo_send, halo_recv, a_send, a_recv, sx_send, sx_recv,
    vu_ssem, vu_rsem, p_ssem, p_rsem, m_ssem, m_rsem, g_ssem, g_rsem, r_ssem, r_rsem,
):
    me = lax.axis_index("region")
    core = lax.axis_index("member")
    q_me = me // NZ
    z = me % NZ
    x = q_me // NY
    y = q_me % NY

    def plane_peer(dx, dy):
        return ((x + dx) % NX) * NY + (y + dy) % NY

    def remote(src, dst, ssem, rsem, region, member):
        return pltpu.make_async_remote_copy(
            src_ref=src, dst_ref=dst, send_sem=ssem, recv_sem=rsem,
            device_id=(region, member), device_id_type=MESH,
        )

    right = (me + 1) % REGIONS
    left = (me + REGIONS - 1) % REGIONS

    edges = [(0, GROUP), (BLOCKS - GROUP, GROUP), (GROUP, BLOCKS - 2 * GROUP)]
    ens_copies = [
        pltpu.make_async_copy(ens_hbm.at[pl.ds(a, n)], ens.at[pl.ds(a, n)], ens_sem.at[i])
        for i, (a, n) in enumerate(edges)
    ]
    for c in ens_copies[:2]:
        c.start()
    cpl_copies = [
        pltpu.make_async_copy(cpl_hbm.at[j], raw.at[j], cpl_sem.at[j]) for j in range(NEIGHB)
    ]
    for c in cpl_copies + ens_copies[2:]:
        c.start()

    barrier = pltpu.get_barrier_semaphore()
    peers = [(plane_peer(dx, dy) * NZ + z, core) for dx, dy in SHIFTS]
    peers += [(q_me * NZ + (z + d) % NZ, core) for d in range(1, NZ)]
    peers += [(me, 1 - core), (right, core), (left, core)]
    for p in peers:
        pl.semaphore_signal(barrier, 1, device_id=p, device_id_type=MESH)
    zero_block = jnp.zeros((1, CELLS, OWN), BF16)
    own0[pl.ds(BLOCKS, 1)] = zero_block
    low[pl.ds(WINDOW, 1)] = zero_block
    high[pl.ds(WINDOW, 1)] = zero_block
    ext1[pl.ds(BLOCKS + 4, 1)] = zero_block

    hit = lax.broadcasted_iota(jnp.int32, (REGIONS, BLOCKS), 0) == dest_row[...]
    numbers = (lax.broadcasted_iota(jnp.int32, (8, BLOCKS), 1) + 1).astype(F32).astype(BF16)
    found = lax.dot_general(
        numbers, jnp.where(hit, 1.0, 0.0).astype(BF16), (((1,), (1,)), ((), ())),
        preferred_element_type=F32,
    )
    inv_rows[...] = jnp.minimum(found, float(BLOCKS)).astype(jnp.int32) - 1
    inv_copy = pltpu.make_async_copy(inv_rows, inv, inv_sem)
    inv_copy.start()

    def cast(a, n):
        own0[pl.ds(a, n)] = ens[pl.ds(a, n)].astype(BF16)

    def to_sides(i, upper, lower, from_left, from_right):
        return [
            remote(upper, from_left, halo_send.at[2 * i], halo_recv.at[2 * i], right, core),
            remote(lower, from_right, halo_send.at[2 * i + 1], halo_recv.at[2 * i + 1], left, core),
        ]

    ens_copies[0].wait()
    cast(0, GROUP)
    ens_copies[1].wait()
    cast(BLOCKS - GROUP, GROUP)
    for pair in range(NEIGHB // 2):
        cpl_copies[2 * pair].wait()
        cpl_copies[2 * pair + 1].wait()

        @pl.loop(0, CELLS // GROUP)
        def _(g):
            for t in range(GROUP):
                c = g * GROUP + t
                slab = raw[pl.ds(2 * pair, 2), c].reshape(2 * CELLS, BLOCKS)
                turned_cpl[pair, pl.ds(pl.multiple_of(c * BLOCKS, 8), BLOCKS)] = slab.T.astype(F32)

    pl.semaphore_wait(barrier, len(peers))
    nbr_send[...] = jnp.zeros_like(nbr_send)
    nbr_send[0:NEIGHB, 0:BLOCKS] = nbr_rows[...]
    sides = to_sides(0, own0.at[pl.ds(BLOCKS - 4, 4)], own0.at[pl.ds(0, 4)],
                     low.at[pl.ds(0, 4)], high.at[pl.ds(4, 4)])
    lists = to_sides(1, nbr_send, nbr_send, nbr_recv.at[0], nbr_recv.at[1])
    for c in lists + sides:
        c.start()
    low[pl.ds(4, 4)] = own0[pl.ds(0, 4)]
    high[pl.ds(0, 4)] = own0[pl.ds(BLOCKS - 4, 4)]

    ens_copies[2].wait()

    @pl.loop(1, BLOCKS // GROUP - 1)
    def _(g):
        cast(g * GROUP, GROUP)


    def couple(i):
        cmat[i] = jnp.concatenate(
            [turned_cpl[pair, pl.ds(i, CELLS, stride=BLOCKS)] for pair in range(NEIGHB // 2)],
            axis=1,
        ).astype(BF16)

    def route(coeff, ext, places):
        return bfdot(coeff, jnp.concatenate([ext[p] for p in places], axis=0))

    for i in (0, 1, BLOCKS - 2, BLOCKS - 1):
        couple(i)
    coeffs = to_sides(2, cmat.at[pl.ds(BLOCKS - 2, 2)], cmat.at[pl.ds(0, 2)],
                      cmat_far.at[pl.ds(0, 2)], cmat_far.at[pl.ds(2, 2)])
    for c in coeffs:
        c.start()

    def inner(i):
        couple(i)
        places = [jnp.clip(nbr[j, i] - HALO, 0, BLOCKS) for j in range(NEIGHB)]
        ext1[i + HALO] = route(cmat[i], own0, places).astype(BF16)

    def inner_group(g):
        for t in range(GROUP):
            inner(HALO + g * GROUP + t)

    pl.loop(0, LISTS_AT)(inner_group)
    for c in lists:
        c.wait()
    far_copy = pltpu.make_async_copy(nbr_recv, nbr_far, far_sem)
    far_copy.start()
    pl.loop(LISTS_AT, (BLOCKS - 4) // GROUP)(inner_group)
    for i in range(HALO + (BLOCKS - 4) // GROUP * GROUP, BLOCKS - HALO):
        inner(i)

    for c in sides:
        c.wait()

    @pl.when(me == 0)
    def _():
        low[pl.ds(0, 4)] = jnp.zeros((4, CELLS, OWN), BF16)

    @pl.when(me == REGIONS - 1)
    def _():
        high[pl.ds(4, 4)] = jnp.zeros((4, CELLS, OWN), BF16)

    def first(e):
        return jnp.clip(e + 2, 0, WINDOW)

    def final(e):
        return jnp.clip(jnp.where(e == BLOCKS + 2 * HALO, WINDOW, e - (BLOCKS - 2)), 0, WINDOW)

    for t in range(HALO):
        i = BLOCKS - HALO + t
        places = [first(nbr[j, t]) for j in range(NEIGHB)]
        ext1[t + HALO] = route(cmat[t], low, places).astype(BF16)
        places = [final(nbr[j, i]) for j in range(NEIGHB)]
        ext1[i + HALO] = route(cmat[i], high, places).astype(BF16)
    for c in coeffs:
        c.wait()
    far_copy.wait()
    for t in range(HALO):
        i = BLOCKS - HALO + t
        places = [final(nbr_far[0, j, i]) for j in range(NEIGHB)]
        ext1[t] = route(cmat_far[t], low, places).astype(BF16)
        places = [first(nbr_far[1, j, t]) for j in range(NEIGHB)]
        ext1[BLOCKS + HALO + t] = route(cmat_far[HALO + t], high, places).astype(BF16)

    @pl.when(me == 0)
    def _():
        ext1[pl.ds(0, HALO)] = jnp.zeros((HALO, CELLS, OWN), BF16)

    @pl.when(me == REGIONS - 1)
    def _():
        ext1[pl.ds(BLOCKS + HALO, HALO)] = jnp.zeros((HALO, CELLS, OWN), BF16)

    inv_copy.wait()

    @pl.loop(0, NZ)
    def _(step):
        k = depth_shift(step, z)
        zr = (z + k) % NZ
        for q in range(NQ):
            r = q * NZ + zr
            b = inv[0, r]
            held = jnp.clip(b, 0, BLOCKS - 1)
            field = route(cmat[held], ext1, [nbr[j, held] for j in range(NEIGHB)])
            field = jnp.where(b >= 0, field, 0.0)
            fc[r] = field
            send[k, q] = field.astype(BF16)
        recv[k, q_me] = send[k, q_me]
        for dx, dy in SHIFTS:
            to = plane_peer(dx, dy)
            remote(send.at[k, to], recv.at[k, q_me], a_send.at[k], a_recv.at[k],
                   to * NZ + z, core).start()

    index = obs_index[...]
    weight = jnp.maximum(0.0, 1.0 - 0.25 * obs_class[...].astype(F32)) / obs_error[...]
    value = weight * obs_value[...]
    place = (index // (CELLS * NZ)) * CELLS + index % CELLS
    plane = (index // CELLS) % NZ
    plane_hit = lax.broadcasted_iota(jnp.int32, (NZ, OBS), 0) == plane

    def three(a):
        hi = a.astype(BF16).astype(F32)
        mid = (a - hi).astype(BF16).astype(F32)
        low = a - hi - mid
        return [hi, mid, low]

    pieces = three(weight) + three(value)
    lhs = jnp.concatenate([jnp.where(plane_hit, p, 0.0) for p in pieces], axis=0).astype(BF16)
    cell_hit = jnp.where(
        lax.broadcasted_iota(jnp.int32, (ROWS, OBS), 0) == place, 1.0, 0.0
    ).astype(BF16)
    sums = lax.dot_general(lhs, cell_hit, (((1,), (1,)), ((), ())), preferred_element_type=F32)
    v_all = sums[0:NZ] + sums[NZ:2 * NZ] + sums[2 * NZ:3 * NZ]
    u_all = sums[3 * NZ:4 * NZ] + sums[4 * NZ:5 * NZ] + sums[5 * NZ:6 * NZ]
    for p in range(NZ):
        for c in range(CHUNKS):
            lanes = slice(c * OWN, (c + 1) * OWN)
            vu_send[p, c:c + 1] = v_all[p:p + 1, lanes]
            vu_send[p, CHUNKS + c:CHUNKS + c + 1] = u_all[p:p + 1, lanes]
    vu_recv[0] = vu_send[z]

    @pl.loop(1, NZ)
    def _(d):
        to = (z + NZ - d) % NZ
        remote(vu_send.at[to], vu_recv.at[d], vu_ssem.at[d], vu_rsem.at[d],
               q_me * NZ + to, core).start()

    ones = jnp.ones((OWN, OWN), BF16)
    eye = (lax.broadcasted_iota(jnp.int32, (OWN, OWN), 0)
           == lax.broadcasted_iota(jnp.int32, (OWN, OWN), 1))

    def start_exchange(k):
        pltpu.make_async_copy(
            recv.at[k, pl.ds(0, NQ - 1)], recv.at[k, pl.ds(0, NQ - 1)], a_recv.at[k]
        ).wait()
        remote(recv.at[k], sib.at[k], sx_send.at[k], sx_recv.at[k], me, 1 - core).start()

    @pl.loop(0, NZ)
    def _(step):
        k = depth_shift(step, z)
        start_exchange(k)
        own = recv[k].reshape(ROWS, OWN)
        total = bfdot(own, ones)
        remote(recv.at[k], sib.at[k], sx_send.at[k], sx_recv.at[k], me, 1 - core).wait()
        other = sib[k].reshape(ROWS, OWN)
        mean = (total + bfdot(other, ones)) * (1.0 / MEMBERS)
        p_own = (own.astype(F32) - mean).astype(BF16)
        p_other = (other.astype(F32) - mean).astype(BF16)
        po[k] = p_own
        ps[k] = p_other
        mean_row = jnp.concatenate(
            [
                jnp.sum(jnp.where(eye, mean[c * OWN:(c + 1) * OWN], 0.0), axis=0, keepdims=True)
                for c in range(ROWS // OWN)
            ],
            axis=1,
        )

        @pl.when(k > 0)
        def _():
            pltpu.make_async_copy(vu_recv.at[k], vu_recv.at[k], vu_rsem.at[k]).wait()

        vu = vu_recv[k]
        v_row = jnp.concatenate([vu[c:c + 1] for c in range(CHUNKS)], axis=1)
        u_row = jnp.concatenate([vu[CHUNKS + c:CHUNKS + c + 1] for c in range(CHUNKS)], axis=1)
        turned = p_own.astype(F32).T
        scaled = (turned * v_row).astype(BF16)
        part_send[k, 0:OWN, 0:OWN] = bfdot(scaled, p_own).astype(BF16)
        part_send[k, 0:OWN, OWN:] = bfdot(scaled, p_other).astype(BF16)
        d_row = u_row - v_row * mean_row
        d_hi = d_row.astype(BF16).astype(F32)
        d_low = d_row - d_hi
        rows16 = lax.broadcasted_iota(jnp.int32, (16, ROWS), 0)
        d_rows = jnp.where(rows16 == 0, d_hi, jnp.where(rows16 == 1, d_low, 0.0)).astype(BF16)

        def tail(p):
            t = jnp.sum(bfdot(d_rows, p), axis=0, keepdims=True)
            hi = t.astype(BF16).astype(F32)
            rows = lax.broadcasted_iota(jnp.int32, (16, OWN), 0)
            return jnp.where(rows == 0, hi, jnp.where(rows == 1, t - hi, 0.0)).astype(BF16)

        part_send[k, OWN:, 0:OWN] = tail(p_own)
        part_send[k, OWN:, OWN:] = tail(p_other)

        @pl.when(k > 0)
        def _():
            remote(part_send.at[k], part_recv.at[k], p_ssem.at[k], p_rsem.at[k],
                   q_me * NZ + (z + k) % NZ, core).start()

    total = part_send[0].astype(F32)
    for k in range(1, NZ):
        pltpu.make_async_copy(part_recv.at[k], part_recv.at[k], p_rsem.at[k]).wait()
        total = total + part_recv[k].astype(F32)
    mx_send[...] = total[0:OWN]
    swap = remote(mx_send, mx_recv, m_ssem, m_rsem, me, 1 - core)
    swap.start()
    innov = jnp.sum(total[OWN:], axis=0, keepdims=True)
    swap.wait()
    crossed = mx_recv[...]
    gram = jnp.concatenate(
        [total[0:OWN], jnp.concatenate([crossed[:, OWN:], crossed[:, :OWN]], axis=1)], axis=0
    )
    identity = jnp.where(
        lax.broadcasted_iota(jnp.int32, (MEMBERS, MEMBERS), 0)
        == lax.broadcasted_iota(jnp.int32, (MEMBERS, MEMBERS), 1), 1.0, 0.0,
    )
    system = (MEMBERS - 1.0) * identity + gram
    frob = jnp.sqrt(jnp.sum(jnp.sum(system * system, axis=0, keepdims=True), axis=1, keepdims=True))
    scaled = system * (1.0 / frob)
    update = 1.5 * identity - 0.5 * scaled
    inverse = halves(update)
    iterate = halves(matmul(halves(scaled), inverse))
    for sweep in range(1, ITERS):
        update = halves(1.5 * identity - 0.5 * matmul(inverse, iterate))
        if sweep < ITERS - 1:
            iterate = halves(matmul(iterate, update))
        last = matmul(update, inverse)
        inverse = halves(last)
    root = last * lax.rsqrt(frob)
    innov8 = jnp.broadcast_to(innov, (8, MEMBERS))
    mean_row = matmul(halves(matmul(halves(innov8), inverse)), inverse)[0:1] * (1.0 / frob)
    mean_col = jnp.broadcast_to(mean_row, (OWN, MEMBERS)).T
    g_recv[0] = (
        mean_col + jnp.sqrt(MEMBERS - 1.0) * root[:, 0:OWN] - identity[:, 0:OWN]
    ).astype(BF16)

    def send_weights(step):
        d = depth_shift(step, z)
        remote(g_recv.at[0], g_recv.at[NZ - d], g_ssem.at[d], g_rsem.at[NZ - d],
               q_me * NZ + (z + d) % NZ, core).start()

    for step in range(NZ - 2, HALF - 1, -1):
        send_weights(step)

    @pl.loop(0, NZ)
    def _(i):
        k = depth_shift(NZ - 1 - i, z)

        @pl.when(k > 0)
        def _():
            pltpu.make_async_copy(g_recv.at[k], g_recv.at[k], g_rsem.at[k]).wait()

        g = g_recv[k]
        incr = bfdot(po[k], g[0:OWN]) + bfdot(ps[k], g[OWN:])
        ret_send[k] = incr.astype(BF16).reshape(NQ, CELLS, OWN)
        r = q_me * NZ + (z + k) % NZ
        ret_recv[r] = ret_send[k, q_me]
        for dx, dy in SHIFTS:
            to = plane_peer(dx, dy)
            remote(ret_send.at[k, to], ret_recv.at[r], r_ssem, r_rsem, to * NZ + z, core).start()

        @pl.when(i == 0)
        def _():
            for step in range(HALF - 1, -1, -1):
                send_weights(step)

    count = NZ * (NQ - 1)
    done = ret_recv.at[pl.ds(0, count)]
    pltpu.make_async_copy(done, done, r_rsem).wait()

    @pl.loop(0, BLOCKS // GROUP)
    def _(g):
        for t in range(GROUP):
            i = g * GROUP + t
            r = dest[i]
            out[i] = (fc[r] + ret_recv[r].astype(F32)).astype(BF16)

    pltpu.make_async_copy(done, done, r_ssem).wait()

    @pl.loop(0, NZ)
    def _(k):
        block = send.at[k, pl.ds(0, NQ - 1)]
        pltpu.make_async_copy(block, block, a_send.at[k]).wait()

        @pl.when(k > 0)
        def _():
            pltpu.make_async_copy(vu_send.at[k], vu_send.at[k], vu_ssem.at[k]).wait()
            pltpu.make_async_copy(part_send.at[k], part_send.at[k], p_ssem.at[k]).wait()
            pltpu.make_async_copy(g_recv.at[k], g_recv.at[k], g_ssem.at[k]).wait()


def shards(
    ensemble, couplings, neighbours, destination, obs_index, obs_class, obs_error, obs_value
):
    smem = pl.BlockSpec(memory_space=pltpu.SMEM)
    vmem = pl.BlockSpec(memory_space=pltpu.VMEM)
    hbm = pl.BlockSpec(memory_space=pl.ANY)
    dma = pltpu.SemaphoreType.DMA
    block = (CELLS, OWN)
    posterior = pl.pallas_call(
        kernel,
        out_shape=pltpu.VMEM((BLOCKS,) + block, BF16),
        in_specs=[smem, vmem, smem, vmem, hbm, hbm, vmem, vmem, vmem, vmem],
        out_specs=vmem,
        scratch_shapes=[
            pltpu.SMEM((8, REGIONS), jnp.int32),
            pltpu.VMEM((8, REGIONS), jnp.int32),
            pltpu.VMEM((BLOCKS,) + block, F32),
            pltpu.VMEM((NEIGHB, CELLS, CELLS, BLOCKS), BF16),
            pltpu.VMEM((NEIGHB // 2, (CELLS + 1) * BLOCKS, 2 * CELLS), F32),
            pltpu.VMEM((BLOCKS, CELLS, NEIGHB * CELLS), BF16),
            pltpu.VMEM((BLOCKS + 1,) + block, BF16),
            pltpu.VMEM((WINDOW + 1,) + block, BF16),
            pltpu.VMEM((WINDOW + 1,) + block, BF16),
            pltpu.VMEM((BLOCKS + 5,) + block, BF16),
            pltpu.VMEM((2 * HALO, CELLS, NEIGHB * CELLS), BF16),
            pltpu.VMEM((8, REGIONS), jnp.int32),
            pltpu.VMEM((2, 8, REGIONS), jnp.int32),
            pltpu.SMEM((2, 8, REGIONS), jnp.int32),
            pltpu.VMEM((REGIONS,) + block, F32),
            pltpu.VMEM((NZ, NQ) + block, BF16),
            pltpu.VMEM((NZ, NQ) + block, BF16),
            pltpu.VMEM((NZ, NQ) + block, BF16),
            pltpu.VMEM((NZ, ROWS, OWN), BF16),
            pltpu.VMEM((NZ, ROWS, OWN), BF16),
            pltpu.VMEM((NZ, NQ) + block, BF16),
            pltpu.VMEM((REGIONS,) + block, BF16),
            pltpu.VMEM((NZ, 2 * CHUNKS, OWN), F32),
            pltpu.VMEM((NZ, 2 * CHUNKS, OWN), F32),
            pltpu.VMEM((NZ, PART, MEMBERS), BF16),
            pltpu.VMEM((NZ, PART, MEMBERS), BF16),
            pltpu.VMEM((OWN, MEMBERS), F32),
            pltpu.VMEM((OWN, MEMBERS), F32),
            pltpu.VMEM((NZ, MEMBERS, OWN), BF16),
            dma((3,)), dma((NEIGHB,)), dma, dma, dma((6,)), dma((6,)),
            dma((NZ,)), dma((NZ,)), dma((NZ,)), dma((NZ,)),
            dma((NZ,)), dma((NZ,)), dma((NZ,)), dma((NZ,)),
            dma, dma, dma((NZ,)), dma((NZ,)), dma, dma,
        ],
        compiler_params=pltpu.CompilerParams(
            collective_id=0, has_side_effects=True, vmem_limit_bytes=58 << 20
        ),
        cost_estimate=pl.CostEstimate(
            flops=4_000_000_000, bytes_accessed=16_000_000, transcendentals=0
        ),
    )(
        neighbours.T, neighbours.T, destination, destination.reshape(1, BLOCKS), ensemble.reshape((BLOCKS,) + block),
        jnp.transpose(couplings, (1, 2, 3, 0)), obs_index, obs_class, obs_error, obs_value,
    )
    return posterior.reshape(BLOCKS * CELLS, OWN)


def solution(mesh):
    return jax.shard_map(
        shards,
        mesh=mesh,
        in_specs=(
            P("region", "member"),
            P("region", None, None, None),
            P("region", None),
            P("region"),
            P("region", None),
            P("region", None),
            P("region", None),
            P("region", None),
        ),
        out_specs=P("region", "member"),
        check_vma=False,
    )
```

```python
import functools
import jax
import jax.numpy as jnp
from jax import lax
from jax.experimental import pallas as pl
from jax.experimental.pallas import tpu as pltpu
from jax.sharding import PartitionSpec as P

MESH = pl.DeviceIdType.MESH
NX, NY, NZ = 4, 4, 8
NQ = NX * NY
REGIONS = NQ * NZ
BLOCKS = 120
CELLS = 64
OWN = 128
MEMBERS = 256
OBS = 512
NEIGHB = 4
ITERS = 4
ROWS = NQ * CELLS
GROUP = 8
HALF = NZ // 2
HALO = 2
WINDOW = 8
LISTS_AT = 11
PART = OWN + 16
CHUNKS = ROWS // OWN
F32 = jnp.float32
BF16 = jnp.bfloat16
SHIFTS = sorted(
    [(a, b) for a in range(NX) for b in range(NY) if (a, b) != (0, 0)],
    key=lambda s: min(s[0], NX - s[0]) + min(s[1], NY - s[1]),
)


def depth_shift(step, z):
    i = NZ - 1 - step
    t = i % HALF
    far = i // HALF
    half = z // HALF
    p = z % HALF
    up = p // 2
    near_place = (p + (1 - 2 * up) * t + HALF) % HALF
    far_place = (1 - up) * (HALF - 1 - t) + up * t
    place = (1 - far) * (half * HALF + near_place) + far * ((1 - half) * HALF + far_place)
    return (place - z + NZ) % NZ


def bfdot(a, b):
    return jnp.dot(a, b, preferred_element_type=F32)


def halves(a):
    hi = a.astype(BF16)
    return hi, (a - hi.astype(F32)).astype(BF16)


def matmul(a, b):
    return bfdot(
        jnp.concatenate([a[0], a[0], a[1]], axis=1), jnp.concatenate([b[0], b[1], b[0]], axis=0)
    )


def kernel(
    nbr, nbr_rows, dest, dest_row, ens_hbm, cpl_hbm, obs_index, obs_class, obs_error, obs_value, out,
    inv, inv_rows, ens, raw, turned_cpl, cmat, own0, low, high, ext1, cmat_far, nbr_send, nbr_recv, nbr_far, fc, send, recv, sib, po, ps, ret_send, ret_recv,
    vu_send, vu_recv, part_send, part_recv, mx_send, mx_recv, g_recv,
    ens_sem, cpl_sem, inv_sem, far_sem, halo_send, halo_recv, a_send, a_recv, sx_send, sx_recv,
    vu_ssem, vu_rsem, p_ssem, p_rsem, m_ssem, m_rsem, g_ssem, g_rsem, r_ssem, r_rsem,
):
    me = lax.axis_index("region")
    core = lax.axis_index("member")
    q_me = me // NZ
    z = me % NZ
    x = q_me // NY
    y = q_me % NY

    def plane_peer(dx, dy):
        return ((x + dx) % NX) * NY + (y + dy) % NY

    def remote(src, dst, ssem, rsem, region, member):
        return pltpu.make_async_remote_copy(
            src_ref=src, dst_ref=dst, send_sem=ssem, recv_sem=rsem,
            device_id=(region, member), device_id_type=MESH,
        )

    right = (me + 1) % REGIONS
    left = (me + REGIONS - 1) % REGIONS

    edges = [(0, GROUP), (BLOCKS - GROUP, GROUP), (GROUP, BLOCKS - 2 * GROUP)]
    ens_copies = [
        pltpu.make_async_copy(ens_hbm.at[pl.ds(a, n)], ens.at[pl.ds(a, n)], ens_sem.at[i])
        for i, (a, n) in enumerate(edges)
    ]
    for c in ens_copies[:2]:
        c.start()
    cpl_copies = [
        pltpu.make_async_copy(cpl_hbm.at[j], raw.at[j], cpl_sem.at[j]) for j in range(NEIGHB)
    ]
    for c in cpl_copies + ens_copies[2:]:
        c.start()

    barrier = pltpu.get_barrier_semaphore()
    peers = [(plane_peer(dx, dy) * NZ + z, core) for dx, dy in SHIFTS]
    peers += [(q_me * NZ + (z + d) % NZ, core) for d in range(1, NZ)]
    peers += [(me, 1 - core), (right, core), (left, core)]
    for p in peers:
        pl.semaphore_signal(barrier, 1, device_id=p, device_id_type=MESH)
    zero_block = jnp.zeros((1, CELLS, OWN), BF16)
    own0[pl.ds(BLOCKS, 1)] = zero_block
    low[pl.ds(WINDOW, 1)] = zero_block
    high[pl.ds(WINDOW, 1)] = zero_block
    ext1[pl.ds(BLOCKS + 4, 1)] = zero_block

    hit = lax.broadcasted_iota(jnp.int32, (REGIONS, BLOCKS), 0) == dest_row[...]
    numbers = (lax.broadcasted_iota(jnp.int32, (8, BLOCKS), 1) + 1).astype(F32).astype(BF16)
    found = lax.dot_general(
        numbers, jnp.where(hit, 1.0, 0.0).astype(BF16), (((1,), (1,)), ((), ())),
        preferred_element_type=F32,
    )
    inv_rows[...] = jnp.minimum(found, float(BLOCKS)).astype(jnp.int32) - 1
    inv_copy = pltpu.make_async_copy(inv_rows, inv, inv_sem)
    inv_copy.start()

    def cast(a, n):
        own0[pl.ds(a, n)] = ens[pl.ds(a, n)].astype(BF16)

    def to_sides(i, upper, lower, from_left, from_right):
        return [
            remote(upper, from_left, halo_send.at[2 * i], halo_recv.at[2 * i], right, core),
            remote(lower, from_right, halo_send.at[2 * i + 1], halo_recv.at[2 * i + 1], left, core),
        ]

    ens_copies[0].wait()
    cast(0, GROUP)
    ens_copies[1].wait()
    cast(BLOCKS - GROUP, GROUP)
    pl.semaphore_wait(barrier, len(peers))
    nbr_send[...] = jnp.zeros_like(nbr_send)
    nbr_send[0:NEIGHB, 0:BLOCKS] = nbr_rows[...]
    sides = to_sides(0, own0.at[pl.ds(BLOCKS - 4, 4)], own0.at[pl.ds(0, 4)],
                     low.at[pl.ds(0, 4)], high.at[pl.ds(4, 4)])
    lists = to_sides(1, nbr_send, nbr_send, nbr_recv.at[0], nbr_recv.at[1])
    for c in lists + sides:
        c.start()
    low[pl.ds(4, 4)] = own0[pl.ds(0, 4)]
    high[pl.ds(0, 4)] = own0[pl.ds(BLOCKS - 4, 4)]

    for pair in range(NEIGHB // 2):
        cpl_copies[2 * pair].wait()
        cpl_copies[2 * pair + 1].wait()

        @pl.loop(0, CELLS // GROUP)
        def _(g):
            for t in range(GROUP):
                c = g * GROUP + t
                slab = raw[pl.ds(2 * pair, 2), c].reshape(2 * CELLS, BLOCKS)
                turned_cpl[pair, pl.ds(pl.multiple_of(c * BLOCKS, 8), BLOCKS)] = slab.T.astype(F32)

    ens_copies[2].wait()

    @pl.loop(1, BLOCKS // GROUP - 1)
    def _(g):
        cast(g * GROUP, GROUP)


    def couple(i):
        cmat[i] = jnp.concatenate(
            [turned_cpl[pair, pl.ds(i, CELLS, stride=BLOCKS)] for pair in range(NEIGHB // 2)],
            axis=1,
        ).astype(BF16)

    def route(coeff, ext, places):
        return bfdot(coeff, jnp.concatenate([ext[p] for p in places], axis=0))

    for i in (0, 1, BLOCKS - 2, BLOCKS - 1):
        couple(i)
    coeffs = to_sides(2, cmat.at[pl.ds(BLOCKS - 2, 2)], cmat.at[pl.ds(0, 2)],
                      cmat_far.at[pl.ds(0, 2)], cmat_far.at[pl.ds(2, 2)])
    for c in coeffs:
        c.start()

    def inner(i):
        couple(i)
        places = [jnp.clip(nbr[j, i] - HALO, 0, BLOCKS) for j in range(NEIGHB)]
        ext1[i + HALO] = route(cmat[i], own0, places).astype(BF16)

    def inner_group(g):
        for t in range(GROUP):
            inner(HALO + g * GROUP + t)

    pl.loop(0, LISTS_AT)(inner_group)
    for c in lists:
        c.wait()
    far_copy = pltpu.make_async_copy(nbr_recv, nbr_far, far_sem)
    far_copy.start()
    pl.loop(LISTS_AT, (BLOCKS - 4) // GROUP)(inner_group)
    for i in range(HALO + (BLOCKS - 4) // GROUP * GROUP, BLOCKS - HALO):
        inner(i)

    for c in sides:
        c.wait()

    @pl.when(me == 0)
    def _():
        low[pl.ds(0, 4)] = jnp.zeros((4, CELLS, OWN), BF16)

    @pl.when(me == REGIONS - 1)
    def _():
        high[pl.ds(4, 4)] = jnp.zeros((4, CELLS, OWN), BF16)

    def first(e):
        return jnp.clip(e + 2, 0, WINDOW)

    def final(e):
        return jnp.clip(jnp.where(e == BLOCKS + 2 * HALO, WINDOW, e - (BLOCKS - 2)), 0, WINDOW)

    for t in range(HALO):
        i = BLOCKS - HALO + t
        places = [first(nbr[j, t]) for j in range(NEIGHB)]
        ext1[t + HALO] = route(cmat[t], low, places).astype(BF16)
        places = [final(nbr[j, i]) for j in range(NEIGHB)]
        ext1[i + HALO] = route(cmat[i], high, places).astype(BF16)
    for c in coeffs:
        c.wait()
    far_copy.wait()
    for t in range(HALO):
        i = BLOCKS - HALO + t
        places = [final(nbr_far[0, j, i]) for j in range(NEIGHB)]
        ext1[t] = route(cmat_far[t], low, places).astype(BF16)
        places = [first(nbr_far[1, j, t]) for j in range(NEIGHB)]
        ext1[BLOCKS + HALO + t] = route(cmat_far[HALO + t], high, places).astype(BF16)

    @pl.when(me == 0)
    def _():
        ext1[pl.ds(0, HALO)] = jnp.zeros((HALO, CELLS, OWN), BF16)

    @pl.when(me == REGIONS - 1)
    def _():
        ext1[pl.ds(BLOCKS + HALO, HALO)] = jnp.zeros((HALO, CELLS, OWN), BF16)

    inv_copy.wait()

    @pl.loop(0, NZ)
    def _(step):
        k = depth_shift(step, z)
        zr = (z + k) % NZ
        for q in range(NQ):
            r = q * NZ + zr
            b = inv[0, r]
            held = jnp.clip(b, 0, BLOCKS - 1)
            field = route(cmat[held], ext1, [nbr[j, held] for j in range(NEIGHB)])
            field = jnp.where(b >= 0, field, 0.0)
            fc[r] = field
            send[k, q] = field.astype(BF16)
        recv[k, q_me] = send[k, q_me]
        for dx, dy in SHIFTS:
            to = plane_peer(dx, dy)
            remote(send.at[k, to], recv.at[k, q_me], a_send.at[k], a_recv.at[k],
                   to * NZ + z, core).start()

    index = obs_index[...]
    weight = jnp.maximum(0.0, 1.0 - 0.25 * obs_class[...].astype(F32)) / obs_error[...]
    value = weight * obs_value[...]
    place = (index // (CELLS * NZ)) * CELLS + index % CELLS
    plane = (index // CELLS) % NZ
    plane_hit = lax.broadcasted_iota(jnp.int32, (NZ, OBS), 0) == plane

    def three(a):
        hi = a.astype(BF16).astype(F32)
        mid = (a - hi).astype(BF16).astype(F32)
        low = a - hi - mid
        return [hi, mid, low]

    pieces = three(weight) + three(value)
    lhs = jnp.concatenate([jnp.where(plane_hit, p, 0.0) for p in pieces], axis=0).astype(BF16)
    cell_hit = jnp.where(
        lax.broadcasted_iota(jnp.int32, (ROWS, OBS), 0) == place, 1.0, 0.0
    ).astype(BF16)
    sums = lax.dot_general(lhs, cell_hit, (((1,), (1,)), ((), ())), preferred_element_type=F32)
    v_all = sums[0:NZ] + sums[NZ:2 * NZ] + sums[2 * NZ:3 * NZ]
    u_all = sums[3 * NZ:4 * NZ] + sums[4 * NZ:5 * NZ] + sums[5 * NZ:6 * NZ]
    for p in range(NZ):
        for c in range(CHUNKS):
            lanes = slice(c * OWN, (c + 1) * OWN)
            vu_send[p, c:c + 1] = v_all[p:p + 1, lanes]
            vu_send[p, CHUNKS + c:CHUNKS + c + 1] = u_all[p:p + 1, lanes]
    vu_recv[0] = vu_send[z]

    @pl.loop(1, NZ)
    def _(d):
        to = (z + NZ - d) % NZ
        remote(vu_send.at[to], vu_recv.at[d], vu_ssem.at[d], vu_rsem.at[d],
               q_me * NZ + to, core).start()

    ones = jnp.ones((OWN, OWN), BF16)
    eye = (lax.broadcasted_iota(jnp.int32, (OWN, OWN), 0)
           == lax.broadcasted_iota(jnp.int32, (OWN, OWN), 1))

    def start_exchange(k):
        pltpu.make_async_copy(
            recv.at[k, pl.ds(0, NQ - 1)], recv.at[k, pl.ds(0, NQ - 1)], a_recv.at[k]
        ).wait()
        remote(recv.at[k], sib.at[k], sx_send.at[k], sx_recv.at[k], me, 1 - core).start()

    @pl.loop(0, NZ)
    def _(step):
        k = depth_shift(step, z)
        start_exchange(k)
        own = recv[k].reshape(ROWS, OWN)
        total = bfdot(own, ones)
        remote(recv.at[k], sib.at[k], sx_send.at[k], sx_recv.at[k], me, 1 - core).wait()
        other = sib[k].reshape(ROWS, OWN)
        mean = (total + bfdot(other, ones)) * (1.0 / MEMBERS)
        p_own = (own.astype(F32) - mean).astype(BF16)
        p_other = (other.astype(F32) - mean).astype(BF16)
        po[k] = p_own
        ps[k] = p_other
        mean_row = jnp.concatenate(
            [
                jnp.sum(jnp.where(eye, mean[c * OWN:(c + 1) * OWN], 0.0), axis=0, keepdims=True)
                for c in range(ROWS // OWN)
            ],
            axis=1,
        )

        @pl.when(k > 0)
        def _():
            pltpu.make_async_copy(vu_recv.at[k], vu_recv.at[k], vu_rsem.at[k]).wait()

        vu = vu_recv[k]
        v_row = jnp.concatenate([vu[c:c + 1] for c in range(CHUNKS)], axis=1)
        u_row = jnp.concatenate([vu[CHUNKS + c:CHUNKS + c + 1] for c in range(CHUNKS)], axis=1)
        turned = p_own.astype(F32).T
        scaled = (turned * v_row).astype(BF16)
        part_send[k, 0:OWN, 0:OWN] = bfdot(scaled, p_own).astype(BF16)
        part_send[k, 0:OWN, OWN:] = bfdot(scaled, p_other).astype(BF16)
        d_row = u_row - v_row * mean_row
        d_hi = d_row.astype(BF16).astype(F32)
        d_low = d_row - d_hi
        rows16 = lax.broadcasted_iota(jnp.int32, (16, ROWS), 0)
        d_rows = jnp.where(rows16 == 0, d_hi, jnp.where(rows16 == 1, d_low, 0.0)).astype(BF16)

        def tail(p):
            t = jnp.sum(bfdot(d_rows, p), axis=0, keepdims=True)
            hi = t.astype(BF16).astype(F32)
            rows = lax.broadcasted_iota(jnp.int32, (16, OWN), 0)
            return jnp.where(rows == 0, hi, jnp.where(rows == 1, t - hi, 0.0)).astype(BF16)

        part_send[k, OWN:, 0:OWN] = tail(p_own)
        part_send[k, OWN:, OWN:] = tail(p_other)

        @pl.when(k > 0)
        def _():
            remote(part_send.at[k], part_recv.at[k], p_ssem.at[k], p_rsem.at[k],
                   q_me * NZ + (z + k) % NZ, core).start()

    total = part_send[0].astype(F32)
    for k in range(1, NZ):
        pltpu.make_async_copy(part_recv.at[k], part_recv.at[k], p_rsem.at[k]).wait()
        total = total + part_recv[k].astype(F32)
    mx_send[...] = total[0:OWN]
    swap = remote(mx_send, mx_recv, m_ssem, m_rsem, me, 1 - core)
    swap.start()
    innov = jnp.sum(total[OWN:], axis=0, keepdims=True)
    swap.wait()
    crossed = mx_recv[...]
    gram = jnp.concatenate(
        [total[0:OWN], jnp.concatenate([crossed[:, OWN:], crossed[:, :OWN]], axis=1)], axis=0
    )
    identity = jnp.where(
        lax.broadcasted_iota(jnp.int32, (MEMBERS, MEMBERS), 0)
        == lax.broadcasted_iota(jnp.int32, (MEMBERS, MEMBERS), 1), 1.0, 0.0,
    )
    system = (MEMBERS - 1.0) * identity + gram
    frob = jnp.sqrt(jnp.sum(jnp.sum(system * system, axis=0, keepdims=True), axis=1, keepdims=True))
    scaled = system * (1.0 / frob)
    update = 1.5 * identity - 0.5 * scaled
    inverse = halves(update)
    iterate = halves(matmul(halves(scaled), inverse))
    for sweep in range(1, ITERS):
        update = halves(1.5 * identity - 0.5 * matmul(inverse, iterate))
        if sweep < ITERS - 1:
            iterate = halves(matmul(iterate, update))
        last = matmul(update, inverse)
        inverse = halves(last)
    root = last * lax.rsqrt(frob)
    innov8 = jnp.broadcast_to(innov, (8, MEMBERS))
    mean_row = matmul(halves(matmul(halves(innov8), inverse)), inverse)[0:1] * (1.0 / frob)
    mean_col = jnp.broadcast_to(mean_row, (OWN, MEMBERS)).T
    g_recv[0] = (
        mean_col + jnp.sqrt(MEMBERS - 1.0) * root[:, 0:OWN] - identity[:, 0:OWN]
    ).astype(BF16)

    def send_weights(step):
        d = depth_shift(step, z)
        remote(g_recv.at[0], g_recv.at[NZ - d], g_ssem.at[d], g_rsem.at[NZ - d],
               q_me * NZ + (z + d) % NZ, core).start()

    for step in range(NZ - 2, HALF - 1, -1):
        send_weights(step)

    @pl.loop(0, NZ)
    def _(i):
        k = depth_shift(NZ - 1 - i, z)

        @pl.when(k > 0)
        def _():
            pltpu.make_async_copy(g_recv.at[k], g_recv.at[k], g_rsem.at[k]).wait()

        g = g_recv[k]
        incr = bfdot(po[k], g[0:OWN]) + bfdot(ps[k], g[OWN:])
        ret_send[k] = incr.astype(BF16).reshape(NQ, CELLS, OWN)
        r = q_me * NZ + (z + k) % NZ
        ret_recv[r] = ret_send[k, q_me]
        for dx, dy in SHIFTS:
            to = plane_peer(dx, dy)
            remote(ret_send.at[k, to], ret_recv.at[r], r_ssem, r_rsem, to * NZ + z, core).start()

        @pl.when(i == 0)
        def _():
            for step in range(HALF - 1, -1, -1):
                send_weights(step)

    count = NZ * (NQ - 1)
    done = ret_recv.at[pl.ds(0, count)]
    pltpu.make_async_copy(done, done, r_rsem).wait()

    @pl.loop(0, BLOCKS // GROUP)
    def _(g):
        for t in range(GROUP):
            i = g * GROUP + t
            r = dest[i]
            out[i] = (fc[r] + ret_recv[r].astype(F32)).astype(BF16)

    pltpu.make_async_copy(done, done, r_ssem).wait()

    @pl.loop(0, NZ)
    def _(k):
        block = send.at[k, pl.ds(0, NQ - 1)]
        pltpu.make_async_copy(block, block, a_send.at[k]).wait()

        @pl.when(k > 0)
        def _():
            pltpu.make_async_copy(vu_send.at[k], vu_send.at[k], vu_ssem.at[k]).wait()
            pltpu.make_async_copy(part_send.at[k], part_send.at[k], p_ssem.at[k]).wait()
            pltpu.make_async_copy(g_recv.at[k], g_recv.at[k], g_ssem.at[k]).wait()


def shards(
    ensemble, couplings, neighbours, destination, obs_index, obs_class, obs_error, obs_value
):
    smem = pl.BlockSpec(memory_space=pltpu.SMEM)
    vmem = pl.BlockSpec(memory_space=pltpu.VMEM)
    hbm = pl.BlockSpec(memory_space=pl.ANY)
    dma = pltpu.SemaphoreType.DMA
    block = (CELLS, OWN)
    posterior = pl.pallas_call(
        kernel,
        out_shape=pltpu.VMEM((BLOCKS,) + block, BF16),
        in_specs=[smem, vmem, smem, vmem, hbm, hbm, vmem, vmem, vmem, vmem],
        out_specs=vmem,
        scratch_shapes=[
            pltpu.SMEM((8, REGIONS), jnp.int32),
            pltpu.VMEM((8, REGIONS), jnp.int32),
            pltpu.VMEM((BLOCKS,) + block, F32),
            pltpu.VMEM((NEIGHB, CELLS, CELLS, BLOCKS), BF16),
            pltpu.VMEM((NEIGHB // 2, (CELLS + 1) * BLOCKS, 2 * CELLS), F32),
            pltpu.VMEM((BLOCKS, CELLS, NEIGHB * CELLS), BF16),
            pltpu.VMEM((BLOCKS + 1,) + block, BF16),
            pltpu.VMEM((WINDOW + 1,) + block, BF16),
            pltpu.VMEM((WINDOW + 1,) + block, BF16),
            pltpu.VMEM((BLOCKS + 5,) + block, BF16),
            pltpu.VMEM((2 * HALO, CELLS, NEIGHB * CELLS), BF16),
            pltpu.VMEM((8, REGIONS), jnp.int32),
            pltpu.VMEM((2, 8, REGIONS), jnp.int32),
            pltpu.SMEM((2, 8, REGIONS), jnp.int32),
            pltpu.VMEM((REGIONS,) + block, F32),
            pltpu.VMEM((NZ, NQ) + block, BF16),
            pltpu.VMEM((NZ, NQ) + block, BF16),
            pltpu.VMEM((NZ, NQ) + block, BF16),
            pltpu.VMEM((NZ, ROWS, OWN), BF16),
            pltpu.VMEM((NZ, ROWS, OWN), BF16),
            pltpu.VMEM((NZ, NQ) + block, BF16),
            pltpu.VMEM((REGIONS,) + block, BF16),
            pltpu.VMEM((NZ, 2 * CHUNKS, OWN), F32),
            pltpu.VMEM((NZ, 2 * CHUNKS, OWN), F32),
            pltpu.VMEM((NZ, PART, MEMBERS), BF16),
            pltpu.VMEM((NZ, PART, MEMBERS), BF16),
            pltpu.VMEM((OWN, MEMBERS), F32),
            pltpu.VMEM((OWN, MEMBERS), F32),
            pltpu.VMEM((NZ, MEMBERS, OWN), BF16),
            dma((3,)), dma((NEIGHB,)), dma, dma, dma((6,)), dma((6,)),
            dma((NZ,)), dma((NZ,)), dma((NZ,)), dma((NZ,)),
            dma((NZ,)), dma((NZ,)), dma((NZ,)), dma((NZ,)),
            dma, dma, dma((NZ,)), dma((NZ,)), dma, dma,
        ],
        compiler_params=pltpu.CompilerParams(
            collective_id=0, has_side_effects=True, vmem_limit_bytes=58 << 20
        ),
        cost_estimate=pl.CostEstimate(
            flops=4_000_000_000, bytes_accessed=16_000_000, transcendentals=0
        ),
    )(
        neighbours.T, neighbours.T, destination, destination.reshape(1, BLOCKS), ensemble.reshape((BLOCKS,) + block),
        jnp.transpose(couplings, (1, 2, 3, 0)), obs_index, obs_class, obs_error, obs_value,
    )
    return posterior.reshape(BLOCKS * CELLS, OWN)


def solution(mesh):
    return jax.shard_map(
        shards,
        mesh=mesh,
        in_specs=(
            P("region", "member"),
            P("region", None, None, None),
            P("region", None),
            P("region"),
            P("region", None),
            P("region", None),
            P("region", None),
            P("region", None),
        ),
        out_specs=P("region", "member"),
        check_vma=False,
    )
```

```python
import functools
import jax
import jax.numpy as jnp
from jax import lax
from jax.experimental import pallas as pl
from jax.experimental.pallas import tpu as pltpu
from jax.sharding import PartitionSpec as P

MESH = pl.DeviceIdType.MESH
NX, NY, NZ = 4, 4, 8
NQ = NX * NY
REGIONS = NQ * NZ
BLOCKS = 120
CELLS = 64
OWN = 128
MEMBERS = 256
OBS = 512
NEIGHB = 4
ITERS = 4
ROWS = NQ * CELLS
GROUP = 8
HALO = 2
WINDOW = 8
PART = OWN + 16
CHUNKS = ROWS // OWN
F32 = jnp.float32
BF16 = jnp.bfloat16
SHIFTS = sorted(
    [(a, b) for a in range(NX) for b in range(NY) if (a, b) != (0, 0)],
    key=lambda s: min(s[0], NX - s[0]) + min(s[1], NY - s[1]),
)


def depth_shift(k):
    return 4 + (1 - 2 * (k % 2)) * ((k + 1) // 2)


def bfdot(a, b):
    return jnp.dot(a, b, preferred_element_type=F32)


def halves(a):
    hi = a.astype(BF16)
    return hi, (a - hi.astype(F32)).astype(BF16)


def matmul(a, b):
    return bfdot(a[0], b[0]) + bfdot(a[0], b[1]) + bfdot(a[1], b[0])


def kernel(
    nbr, nbr_rows, dest, dest_row, ens_hbm, cpl_hbm, obs_index, obs_class, obs_error, obs_value, out,
    inv, inv_rows, ens, raw, turned_cpl, cmat, own0, low, high, ext1, cmat_far, nbr_send, nbr_recv, nbr_far, fc, send, recv, sib, po, ps, ret_send, ret_recv,
    vu_send, vu_recv, part_send, part_recv, mx_send, mx_recv, g_recv,
    ens_sem, cpl_sem, inv_sem, far_sem, halo_send, halo_recv, a_send, a_recv, sx_send, sx_recv,
    vu_ssem, vu_rsem, p_ssem, p_rsem, m_ssem, m_rsem, g_ssem, g_rsem, r_ssem, r_rsem,
):
    me = lax.axis_index("region")
    core = lax.axis_index("member")
    q_me = me // NZ
    z = me % NZ
    x = q_me // NY
    y = q_me % NY

    def plane_peer(dx, dy):
        return ((x + dx) % NX) * NY + (y + dy) % NY

    def remote(src, dst, ssem, rsem, region, member):
        return pltpu.make_async_remote_copy(
            src_ref=src, dst_ref=dst, send_sem=ssem, recv_sem=rsem,
            device_id=(region, member), device_id_type=MESH,
        )

    right = (me + 1) % REGIONS
    left = (me + REGIONS - 1) % REGIONS

    edges = [(0, GROUP), (BLOCKS - GROUP, GROUP), (GROUP, BLOCKS - 2 * GROUP)]
    ens_copies = [
        pltpu.make_async_copy(ens_hbm.at[pl.ds(a, n)], ens.at[pl.ds(a, n)], ens_sem.at[i])
        for i, (a, n) in enumerate(edges)
    ]
    for c in ens_copies[:2]:
        c.start()
    cpl_copies = [
        pltpu.make_async_copy(cpl_hbm.at[j], raw.at[j], cpl_sem.at[j]) for j in range(NEIGHB)
    ]
    barrier = pltpu.get_barrier_semaphore()
    peers = [(plane_peer(dx, dy) * NZ + z, core) for dx, dy in SHIFTS]
    peers += [(q_me * NZ + (z + d) % NZ, core) for d in range(1, NZ)]
    peers += [(me, 1 - core), (right, core), (left, core)]
    for p in peers:
        pl.semaphore_signal(barrier, 1, device_id=p, device_id_type=MESH)
    for c in cpl_copies + ens_copies[2:]:
        c.start()

    nbr_send[...] = jnp.zeros_like(nbr_send)
    nbr_send[0:NEIGHB, 0:BLOCKS] = nbr_rows[...]
    zero_block = jnp.zeros((1, CELLS, OWN), BF16)
    own0[pl.ds(BLOCKS, 1)] = zero_block
    low[pl.ds(WINDOW, 1)] = zero_block
    high[pl.ds(WINDOW, 1)] = zero_block
    ext1[pl.ds(BLOCKS + 4, 1)] = zero_block

    def cast(a, n):
        own0[pl.ds(a, n)] = ens[pl.ds(a, n)].astype(BF16)

    def to_sides(i, upper, lower, from_left, from_right):
        return [
            remote(upper, from_left, halo_send.at[2 * i], halo_recv.at[2 * i], right, core),
            remote(lower, from_right, halo_send.at[2 * i + 1], halo_recv.at[2 * i + 1], left, core),
        ]

    ens_copies[0].wait()
    cast(0, GROUP)
    ens_copies[1].wait()
    cast(BLOCKS - GROUP, GROUP)
    pl.semaphore_wait(barrier, len(peers))
    sides = to_sides(0, own0.at[pl.ds(BLOCKS - 4, 4)], own0.at[pl.ds(0, 4)],
                     low.at[pl.ds(0, 4)], high.at[pl.ds(4, 4)])
    lists = to_sides(1, nbr_send, nbr_send, nbr_recv.at[0], nbr_recv.at[1])
    for c in sides + lists:
        c.start()
    low[pl.ds(4, 4)] = own0[pl.ds(0, 4)]
    high[pl.ds(0, 4)] = own0[pl.ds(BLOCKS - 4, 4)]

    hit = lax.broadcasted_iota(jnp.int32, (REGIONS, BLOCKS), 0) == dest_row[...]
    numbers = (lax.broadcasted_iota(jnp.int32, (8, BLOCKS), 1) + 1).astype(F32).astype(BF16)
    found = lax.dot_general(
        numbers, jnp.where(hit, 1.0, 0.0).astype(BF16), (((1,), (1,)), ((), ())),
        preferred_element_type=F32,
    )
    inv_rows[...] = jnp.minimum(found, float(BLOCKS)).astype(jnp.int32) - 1
    inv_copy = pltpu.make_async_copy(inv_rows, inv, inv_sem)
    inv_copy.start()

    for pair in range(NEIGHB // 2):
        cpl_copies[2 * pair].wait()
        cpl_copies[2 * pair + 1].wait()

        @pl.loop(0, CELLS // GROUP)
        def _(g):
            for t in range(GROUP):
                c = g * GROUP + t
                slab = raw[pl.ds(2 * pair, 2), c].reshape(2 * CELLS, BLOCKS)
                turned_cpl[pair, pl.ds(pl.multiple_of(c * BLOCKS, 8), BLOCKS)] = slab.T.astype(F32)

    ens_copies[2].wait()

    @pl.loop(1, BLOCKS // GROUP - 1)
    def _(g):
        cast(g * GROUP, GROUP)


    def couple(i):
        cmat[i] = jnp.concatenate(
            [turned_cpl[pair, pl.ds(i, CELLS, stride=BLOCKS)] for pair in range(NEIGHB // 2)],
            axis=1,
        ).astype(BF16)

    def route(coeff, ext, places):
        return bfdot(coeff, jnp.concatenate([ext[p] for p in places], axis=0))

    for i in (0, 1, BLOCKS - 2, BLOCKS - 1):
        couple(i)
    coeffs = to_sides(2, cmat.at[pl.ds(BLOCKS - 2, 2)], cmat.at[pl.ds(0, 2)],
                      cmat_far.at[pl.ds(0, 2)], cmat_far.at[pl.ds(2, 2)])
    for c in coeffs:
        c.start()

    def inner(i):
        couple(i)
        places = [jnp.clip(nbr[j, i] - HALO, 0, BLOCKS) for j in range(NEIGHB)]
        ext1[i + HALO] = route(cmat[i], own0, places).astype(BF16)

    @pl.loop(0, (BLOCKS - 4) // GROUP)
    def _(g):
        for t in range(GROUP):
            inner(HALO + g * GROUP + t)

    for i in range(HALO + (BLOCKS - 4) // GROUP * GROUP, BLOCKS - HALO):
        inner(i)

    for c in lists:
        c.wait()
    far_copy = pltpu.make_async_copy(nbr_recv, nbr_far, far_sem)
    far_copy.start()
    for c in sides:
        c.wait()

    @pl.when(me == 0)
    def _():
        low[pl.ds(0, 4)] = jnp.zeros((4, CELLS, OWN), BF16)

    @pl.when(me == REGIONS - 1)
    def _():
        high[pl.ds(4, 4)] = jnp.zeros((4, CELLS, OWN), BF16)

    def first(e):
        return jnp.clip(e + 2, 0, WINDOW)

    def final(e):
        return jnp.clip(jnp.where(e == BLOCKS + 2 * HALO, WINDOW, e - (BLOCKS - 2)), 0, WINDOW)

    for t in range(HALO):
        i = BLOCKS - HALO + t
        places = [first(nbr[j, t]) for j in range(NEIGHB)]
        ext1[t + HALO] = route(cmat[t], low, places).astype(BF16)
        places = [final(nbr[j, i]) for j in range(NEIGHB)]
        ext1[i + HALO] = route(cmat[i], high, places).astype(BF16)
    for c in coeffs:
        c.wait()
    far_copy.wait()
    for t in range(HALO):
        i = BLOCKS - HALO + t
        places = [final(nbr_far[0, j, i]) for j in range(NEIGHB)]
        ext1[t] = route(cmat_far[t], low, places).astype(BF16)
        places = [first(nbr_far[1, j, t]) for j in range(NEIGHB)]
        ext1[BLOCKS + HALO + t] = route(cmat_far[HALO + t], high, places).astype(BF16)

    @pl.when(me == 0)
    def _():
        ext1[pl.ds(0, HALO)] = jnp.zeros((HALO, CELLS, OWN), BF16)

    @pl.when(me == REGIONS - 1)
    def _():
        ext1[pl.ds(BLOCKS + HALO, HALO)] = jnp.zeros((HALO, CELLS, OWN), BF16)

    inv_copy.wait()

    @pl.loop(0, NZ)
    def _(k):
        zr = (z + depth_shift(k)) % NZ
        for q in range(NQ):
            r = q * NZ + zr
            b = inv[0, r]
            held = jnp.clip(b, 0, BLOCKS - 1)
            field = route(cmat[held], ext1, [nbr[j, held] for j in range(NEIGHB)])
            field = jnp.where(b >= 0, field, 0.0)
            fc[r] = field
            send[k, q] = field.astype(BF16)
        recv[k, q_me] = send[k, q_me]
        for dx, dy in SHIFTS:
            to = plane_peer(dx, dy)
            remote(send.at[k, to], recv.at[k, q_me], a_send.at[k], a_recv.at[k],
                   to * NZ + z, core).start()

    index = obs_index[...]
    weight = jnp.maximum(0.0, 1.0 - 0.25 * obs_class[...].astype(F32)) / obs_error[...]
    value = weight * obs_value[...]
    place = (index // (CELLS * NZ)) * CELLS + index % CELLS
    plane = (index // CELLS) % NZ
    plane_hit = lax.broadcasted_iota(jnp.int32, (NZ, OBS), 0) == plane

    def three(a):
        hi = a.astype(BF16).astype(F32)
        mid = (a - hi).astype(BF16).astype(F32)
        low = a - hi - mid
        return [hi, mid, low]

    pieces = three(weight) + three(value)
    lhs = jnp.concatenate([jnp.where(plane_hit, p, 0.0) for p in pieces], axis=0).astype(BF16)
    cell_hit = jnp.where(
        lax.broadcasted_iota(jnp.int32, (ROWS, OBS), 0) == place, 1.0, 0.0
    ).astype(BF16)
    sums = lax.dot_general(lhs, cell_hit, (((1,), (1,)), ((), ())), preferred_element_type=F32)
    v_all = sums[0:NZ] + sums[NZ:2 * NZ] + sums[2 * NZ:3 * NZ]
    u_all = sums[3 * NZ:4 * NZ] + sums[4 * NZ:5 * NZ] + sums[5 * NZ:6 * NZ]
    for p in range(NZ):
        for c in range(CHUNKS):
            lanes = slice(c * OWN, (c + 1) * OWN)
            vu_send[p, c:c + 1] = v_all[p:p + 1, lanes]
            vu_send[p, CHUNKS + c:CHUNKS + c + 1] = u_all[p:p + 1, lanes]
    vu_recv[NZ - 1] = vu_send[z]

    @pl.loop(0, NZ - 1)
    def _(k):
        to = (z + NZ - depth_shift(k)) % NZ
        remote(vu_send.at[to], vu_recv.at[k], vu_ssem.at[k], vu_rsem.at[k],
               q_me * NZ + to, core).start()

    ones = jnp.ones((OWN, OWN), BF16)
    eye = (lax.broadcasted_iota(jnp.int32, (OWN, OWN), 0)
           == lax.broadcasted_iota(jnp.int32, (OWN, OWN), 1))

    def start_exchange(k):
        pltpu.make_async_copy(
            recv.at[k, pl.ds(0, NQ - 1)], recv.at[k, pl.ds(0, NQ - 1)], a_recv.at[k]
        ).wait()
        remote(recv.at[k], sib.at[k], sx_send.at[k], sx_recv.at[k], me, 1 - core).start()

    @pl.loop(0, NZ)
    def _(k):
        start_exchange(k)
        own = recv[k].reshape(ROWS, OWN)
        total = bfdot(own, ones)
        remote(recv.at[k], sib.at[k], sx_send.at[k], sx_recv.at[k], me, 1 - core).wait()
        other = sib[k].reshape(ROWS, OWN)
        mean = (total + bfdot(other, ones)) * (1.0 / MEMBERS)
        p_own = (own.astype(F32) - mean).astype(BF16)
        p_other = (other.astype(F32) - mean).astype(BF16)
        po[k] = p_own
        ps[k] = p_other
        mean_row = jnp.concatenate(
            [
                jnp.sum(jnp.where(eye, mean[c * OWN:(c + 1) * OWN], 0.0), axis=0, keepdims=True)
                for c in range(ROWS // OWN)
            ],
            axis=1,
        )

        @pl.when(k < NZ - 1)
        def _():
            pltpu.make_async_copy(vu_recv.at[k], vu_recv.at[k], vu_rsem.at[k]).wait()

        vu = vu_recv[k]
        v_row = jnp.concatenate([vu[c:c + 1] for c in range(CHUNKS)], axis=1)
        u_row = jnp.concatenate([vu[CHUNKS + c:CHUNKS + c + 1] for c in range(CHUNKS)], axis=1)
        turned = p_own.astype(F32).T
        scaled = (turned * v_row).astype(BF16)
        part_send[k, 0:OWN, 0:OWN] = bfdot(scaled, p_own).astype(BF16)
        part_send[k, 0:OWN, OWN:] = bfdot(scaled, p_other).astype(BF16)
        d_row = u_row - v_row * mean_row
        d_hi = d_row.astype(BF16).astype(F32)
        d_low = d_row - d_hi
        rows16 = lax.broadcasted_iota(jnp.int32, (16, ROWS), 0)
        d_rows = jnp.where(rows16 == 0, d_hi, jnp.where(rows16 == 1, d_low, 0.0)).astype(BF16)

        def tail(p):
            t = jnp.sum(bfdot(d_rows, p), axis=0, keepdims=True)
            hi = t.astype(BF16).astype(F32)
            rows = lax.broadcasted_iota(jnp.int32, (16, OWN), 0)
            return jnp.where(rows == 0, hi, jnp.where(rows == 1, t - hi, 0.0)).astype(BF16)

        part_send[k, OWN:, 0:OWN] = tail(p_own)
        part_send[k, OWN:, OWN:] = tail(p_other)

        @pl.when(k < NZ - 1)
        def _():
            remote(part_send.at[k], part_recv.at[k], p_ssem.at[k], p_rsem.at[k],
                   q_me * NZ + (z + depth_shift(k)) % NZ, core).start()

    total = part_send[NZ - 1].astype(F32)
    for k in range(NZ - 1):
        pltpu.make_async_copy(part_recv.at[k], part_recv.at[k], p_rsem.at[k]).wait()
        total = total + part_recv[k].astype(F32)
    mx_send[...] = total[0:OWN]
    swap = remote(mx_send, mx_recv, m_ssem, m_rsem, me, 1 - core)
    swap.start()
    innov = jnp.sum(total[OWN:], axis=0, keepdims=True)
    swap.wait()
    crossed = mx_recv[...]
    gram = jnp.concatenate(
        [total[0:OWN], jnp.concatenate([crossed[:, OWN:], crossed[:, :OWN]], axis=1)], axis=0
    )
    identity = jnp.where(
        lax.broadcasted_iota(jnp.int32, (MEMBERS, MEMBERS), 0)
        == lax.broadcasted_iota(jnp.int32, (MEMBERS, MEMBERS), 1), 1.0, 0.0,
    )
    system = (MEMBERS - 1.0) * identity + gram
    frob = jnp.sqrt(jnp.sum(jnp.sum(system * system, axis=0, keepdims=True), axis=1, keepdims=True))
    scaled = system * (1.0 / frob)
    update = 1.5 * identity - 0.5 * scaled
    inverse = halves(update)
    iterate = halves(matmul(halves(scaled), inverse))
    for sweep in range(1, ITERS):
        update = halves(1.5 * identity - 0.5 * matmul(inverse, iterate))
        if sweep < ITERS - 1:
            iterate = halves(matmul(iterate, update))
        last = matmul(update, inverse)
        inverse = halves(last)
    root = last * lax.rsqrt(frob)
    innov8 = jnp.broadcast_to(innov, (8, MEMBERS))
    mean_row = matmul(halves(matmul(halves(innov8), inverse)), inverse)[0:1] * (1.0 / frob)
    mean_col = jnp.broadcast_to(mean_row, (OWN, MEMBERS)).T
    g_recv[NZ - 1] = (
        mean_col + jnp.sqrt(MEMBERS - 1.0) * root[:, 0:OWN] - identity[:, 0:OWN]
    ).astype(BF16)

    def send_weights(k):
        remote(g_recv.at[NZ - 1], g_recv.at[k], g_ssem.at[k], g_rsem.at[k],
               q_me * NZ + (z + NZ - depth_shift(k)) % NZ, core).start()

    send_weights(NZ - 2)
    send_weights(NZ - 3)

    @pl.loop(0, NZ)
    def _(i):
        k = NZ - 1 - i

        @pl.when(k < NZ - 1)
        def _():
            pltpu.make_async_copy(g_recv.at[k], g_recv.at[k], g_rsem.at[k]).wait()

        g = g_recv[k]
        incr = bfdot(po[k], g[0:OWN]) + bfdot(ps[k], g[OWN:])
        ret_send[k] = incr.astype(BF16).reshape(NQ, CELLS, OWN)
        r = q_me * NZ + (z + depth_shift(k)) % NZ
        ret_recv[r] = ret_send[k, q_me]
        for dx, dy in SHIFTS:
            to = plane_peer(dx, dy)
            remote(ret_send.at[k, to], ret_recv.at[r], r_ssem, r_rsem, to * NZ + z, core).start()

        @pl.when(i < 2)
        def _():
            send_weights(NZ - 4 - 2 * i)
            send_weights(NZ - 5 - 2 * i)

        @pl.when(i == 2)
        def _():
            send_weights(0)

    count = NZ * (NQ - 1)
    done = ret_recv.at[pl.ds(0, count)]
    pltpu.make_async_copy(done, done, r_rsem).wait()

    @pl.loop(0, BLOCKS // GROUP)
    def _(g):
        for t in range(GROUP):
            i = g * GROUP + t
            r = dest[i]
            out[i] = (fc[r] + ret_recv[r].astype(F32)).astype(BF16)

    pltpu.make_async_copy(done, done, r_ssem).wait()

    @pl.loop(0, NZ)
    def _(k):
        block = send.at[k, pl.ds(0, NQ - 1)]
        pltpu.make_async_copy(block, block, a_send.at[k]).wait()

        @pl.when(k < NZ - 1)
        def _():
            pltpu.make_async_copy(vu_send.at[k], vu_send.at[k], vu_ssem.at[k]).wait()
            pltpu.make_async_copy(part_send.at[k], part_send.at[k], p_ssem.at[k]).wait()
            pltpu.make_async_copy(g_recv.at[k], g_recv.at[k], g_ssem.at[k]).wait()


def shards(
    ensemble, couplings, neighbours, destination, obs_index, obs_class, obs_error, obs_value
):
    smem = pl.BlockSpec(memory_space=pltpu.SMEM)
    vmem = pl.BlockSpec(memory_space=pltpu.VMEM)
    hbm = pl.BlockSpec(memory_space=pl.ANY)
    dma = pltpu.SemaphoreType.DMA
    block = (CELLS, OWN)
    posterior = pl.pallas_call(
        kernel,
        out_shape=pltpu.VMEM((BLOCKS,) + block, BF16),
        in_specs=[smem, vmem, smem, vmem, hbm, hbm, vmem, vmem, vmem, vmem],
        out_specs=vmem,
        scratch_shapes=[
            pltpu.SMEM((8, REGIONS), jnp.int32),
            pltpu.VMEM((8, REGIONS), jnp.int32),
            pltpu.VMEM((BLOCKS,) + block, F32),
            pltpu.VMEM((NEIGHB, CELLS, CELLS, BLOCKS), BF16),
            pltpu.VMEM((NEIGHB // 2, (CELLS + 1) * BLOCKS, 2 * CELLS), F32),
            pltpu.VMEM((BLOCKS, CELLS, NEIGHB * CELLS), BF16),
            pltpu.VMEM((BLOCKS + 1,) + block, BF16),
            pltpu.VMEM((WINDOW + 1,) + block, BF16),
            pltpu.VMEM((WINDOW + 1,) + block, BF16),
            pltpu.VMEM((BLOCKS + 5,) + block, BF16),
            pltpu.VMEM((2 * HALO, CELLS, NEIGHB * CELLS), BF16),
            pltpu.VMEM((8, REGIONS), jnp.int32),
            pltpu.VMEM((2, 8, REGIONS), jnp.int32),
            pltpu.SMEM((2, 8, REGIONS), jnp.int32),
            pltpu.VMEM((REGIONS,) + block, F32),
            pltpu.VMEM((NZ, NQ) + block, BF16),
            pltpu.VMEM((NZ, NQ) + block, BF16),
            pltpu.VMEM((NZ, NQ) + block, BF16),
            pltpu.VMEM((NZ, ROWS, OWN), BF16),
            pltpu.VMEM((NZ, ROWS, OWN), BF16),
            pltpu.VMEM((NZ, NQ) + block, BF16),
            pltpu.VMEM((REGIONS,) + block, BF16),
            pltpu.VMEM((NZ, 2 * CHUNKS, OWN), F32),
            pltpu.VMEM((NZ, 2 * CHUNKS, OWN), F32),
            pltpu.VMEM((NZ, PART, MEMBERS), BF16),
            pltpu.VMEM((NZ - 1, PART, MEMBERS), BF16),
            pltpu.VMEM((OWN, MEMBERS), F32),
            pltpu.VMEM((OWN, MEMBERS), F32),
            pltpu.VMEM((NZ, MEMBERS, OWN), BF16),
            dma((3,)), dma((NEIGHB,)), dma, dma, dma((6,)), dma((6,)),
            dma((NZ,)), dma((NZ,)), dma((NZ,)), dma((NZ,)),
            dma((NZ,)), dma((NZ,)), dma((NZ,)), dma((NZ,)),
            dma, dma, dma((NZ,)), dma((NZ,)), dma, dma,
        ],
        compiler_params=pltpu.CompilerParams(
            collective_id=0, has_side_effects=True, vmem_limit_bytes=58 << 20
        ),
        cost_estimate=pl.CostEstimate(
            flops=4_000_000_000, bytes_accessed=16_000_000, transcendentals=0
        ),
    )(
        neighbours.T, neighbours.T, destination, destination.reshape(1, BLOCKS), ensemble.reshape((BLOCKS,) + block),
        jnp.transpose(couplings, (1, 2, 3, 0)), obs_index, obs_class, obs_error, obs_value,
    )
    return posterior.reshape(BLOCKS * CELLS, OWN)


def solution(mesh):
    return jax.shard_map(
        shards,
        mesh=mesh,
        in_specs=(
            P("region", "member"),
            P("region", None, None, None),
            P("region", None),
            P("region"),
            P("region", None),
            P("region", None),
            P("region", None),
            P("region", None),
        ),
        out_specs=P("region", "member"),
        check_vma=False,
    )
```
